32 devices in a mesh: rep: 2 (over core), ty: 4 (over z), tx: 4 (over y, x).
Axes of the slice: x: 2, y: 2, z: 4, core: 2. Of those that a mesh axis runs over, the one named last changes fastest.
Arguments:
- tokens: bfloat16 [2, 256, 16, 512], P('rep', 'ty', 'tx'), may hold values from -160 to 160
- qkv_weight: bfloat16 [512, 1536], replicated, may hold values from -16 to 16
- cotangent: bfloat16 [2, 256, 16, 512], P('rep', 'ty', 'tx'), may hold values from -6 to 6
Outputs:
- token_grad: bfloat16 [2, 256, 16, 512], P('rep', 'ty', 'tx')
- weight_grad: float32 [512, 1536], P(('ty', 'tx'))
The draws below stay inside these ranges and needn't reach their ends.
All inputs are finite; a program needn't handle non-finite values.
Results may differ from the reference program's by a relative error of at most 0.024.
Values may be sent and summed in bfloat16 or wider, within the bound.
No kernel may reach another device: no remote copies, remote signals or barrier semaphores. Data moves between devices by JAX's collectives and lax.ppermute only.
A program may use at most 64 MiB of HBM per device.

```python
import math
import jax
import jax.numpy as jnp
from jax import lax

D = 512
HEADS = 16
HEAD_DIM = 32
GRID = 8
TH = 64
TW = 4
REPS = 2
HEIGHT = 256
WIDTH = 16
N_REP = 2
N_TY = 4
N_TX = 4


def draw_tokens(key, part):
    key_list = jax.random.split(key, 4)
    full_shape = (REPS, HEIGHT, WIDTH, D)
    base_draw = jax.random.truncated_normal(key_list[0], -4.0, 4.0, full_shape, jnp.float32)
    log_low = math.log(0.3)
    log_high = math.log(3.0)
    pixel_scale = jnp.exp(jax.random.uniform(key_list[1], (REPS, HEIGHT, WIDTH, 1), jnp.float32, log_low, log_high))
    channel_scale = jnp.exp(jax.random.uniform(key_list[2], (1, 1, 1, D), jnp.float32, log_low, log_high))
    tile_total = HEIGHT // TH * (WIDTH // TW)
    tile_ids = (jnp.arange(HEIGHT) // TH)[:, None] * (WIDTH // TW) + (jnp.arange(WIDTH) // TW)[None, :]
    orders = jax.vmap(lambda subkey: jax.random.permutation(subkey, tile_total))(jax.random.split(key_list[3], REPS))
    targets = orders[:, tile_ids]
    blocks = jnp.arange(D) // (D // tile_total)
    boost_factor = jnp.where(targets[..., None] == blocks, 4.0, 1.0)
    values = base_draw * pixel_scale * channel_scale * boost_factor
    return values.astype(jnp.bfloat16)


def draw_qkv_weight(key, part):
    key_list = jax.random.split(key, 1)
    return (jax.random.truncated_normal(key_list[0], -3.0, 3.0, (D, 3 * D), jnp.float32) * D ** (-0.5)).astype(jnp.bfloat16)


def block_levels(key, dims, pieces, low, top_value):
    loudness = 1.0
    for dim, blocks in pieces:
        steps = jax.random.uniform(jax.random.fold_in(jax.random.fold_in(key, 6), dim), (blocks,), jnp.float32, low / len(pieces), top_value / len(pieces))
        loudness = loudness * jnp.repeat(jnp.exp(steps), dims[dim] // blocks).reshape((-1,) + (1,) * (len(dims) - 1 - dim))
    return loudness


def scatter_about(rng, extent, width, bound, cuts=(), dtype=jnp.bfloat16):
    values = jax.random.normal(rng, extent, jnp.float32) * width
    if len(cuts) > 0:
        values = block_levels(rng, extent, cuts, -0.22, 0.18) * values
    return jnp.clip(values, min=-bound, max=bound).astype(dtype)


def setup_inputs(seed: int = 0) -> dict:
    arg_keys = jax.random.split(jax.random.key(seed), 4)
    return {
        "tokens": draw_tokens(jax.random.fold_in(arg_keys[3], 71), 0),
        "qkv_weight": draw_qkv_weight(jax.random.fold_in(arg_keys[3], 71), 0),
        "cotangent": scatter_about(arg_keys[2], (REPS, HEIGHT, WIDTH, D), 1.0, 6.0, ((0, 2), (1, 4), (2, 4))),
    }


eps_norm = 1e-05

def normalize(values):
    center = values - lax.optimization_barrier(jnp.mean(values, axis=-1, keepdims=True))
    inv_std = lax.rsqrt(lax.optimization_barrier(jnp.mean(center * center, axis=-1, keepdims=True)) + eps_norm)
    return (center * inv_std, inv_std)

def window_grads(window_x, window_g, qkv_weight):
    win_count, win_tokens, channels = window_x.shape
    standard, inv_std = normalize(window_x.astype(jnp.float32))
    normed = standard.astype(jnp.bfloat16).reshape(win_count * win_tokens, channels)
    projection = jnp.dot(normed, qkv_weight, preferred_element_type=jnp.float32)
    head_shape = (win_count, win_tokens, HEADS, HEAD_DIM)
    query_heads = (projection[:, :channels] * HEAD_DIM ** (-0.5)).astype(jnp.bfloat16).reshape(head_shape)
    key_heads = projection[:, channels:2 * channels].astype(jnp.bfloat16).reshape(head_shape)
    value_heads = projection[:, 2 * channels:].astype(jnp.bfloat16).reshape(head_shape)
    query_wide = query_heads.astype(jnp.float32)
    key_wide = key_heads.astype(jnp.float32)
    value_wide = value_heads.astype(jnp.float32)
    scores = jnp.einsum('wqne,wkne->wnqk', query_wide, key_wide)
    peak_score = lax.optimization_barrier(jnp.max(scores, axis=-1, keepdims=True))
    exponent = jnp.exp(scores - peak_score)
    attn_probs = exponent / lax.optimization_barrier(jnp.sum(exponent, axis=-1, keepdims=True))
    probs_low = attn_probs.astype(jnp.bfloat16)
    grad_heads = window_g.astype(jnp.float32).reshape(head_shape)
    attn_grad = jnp.einsum('wqne,wkne->wnqk', grad_heads, value_wide)
    value_grad = jnp.einsum('wnqk,wqne->wkne', probs_low.astype(jnp.float32), grad_heads).astype(jnp.bfloat16)
    score_grad = (attn_probs * (attn_grad - lax.optimization_barrier(jnp.sum(attn_probs * attn_grad, axis=-1, keepdims=True)))).astype(jnp.bfloat16)
    score_wide = score_grad.astype(jnp.float32)
    query_grad = (jnp.einsum('wnqk,wkne->wqne', score_wide, key_wide) * HEAD_DIM ** (-0.5)).astype(jnp.bfloat16)
    key_grad = jnp.einsum('wnqk,wqne->wkne', score_wide, query_wide).astype(jnp.bfloat16)
    flat_shape = (win_count * win_tokens, channels)
    proj_grad = jnp.concatenate([query_grad.reshape(flat_shape), key_grad.reshape(flat_shape), value_grad.reshape(flat_shape)], axis=1)
    normed_grad = lax.dot_general(proj_grad, qkv_weight, (((1,), (1,)), ((), ())), preferred_element_type=jnp.float32)
    normed_grad = normed_grad.reshape(win_count, win_tokens, channels)
    weight_term = lax.dot_general(normed, proj_grad, (((0,), (0,)), ((), ())), preferred_element_type=jnp.float32)
    inner_term = normed_grad - lax.optimization_barrier(jnp.mean(normed_grad, axis=-1, keepdims=True)) - standard * lax.optimization_barrier(jnp.mean(normed_grad * standard, axis=-1, keepdims=True))
    token_grad = (window_g.astype(jnp.float32) + inv_std * inner_term).astype(jnp.bfloat16)
    return (token_grad, weight_term)

def reference(tokens, qkv_weight, cotangent):
    stride_rows = HEIGHT // GRID
    stride_cols = WIDTH // GRID

    def to_windows(values):
        return values.reshape(GRID, stride_rows, GRID, stride_cols, D).transpose(1, 3, 0, 2, 4).reshape(stride_rows * stride_cols, GRID * GRID, D)

    def from_windows(values):
        return values.reshape(stride_rows, stride_cols, GRID, GRID, D).transpose(2, 0, 3, 1, 4).reshape(HEIGHT, WIDTH, D)

    def one_sample(sample):
        sample_x, sample_g = sample
        grad_windows, weight_term = window_grads(to_windows(sample_x), to_windows(sample_g), qkv_weight)
        return (from_windows(grad_windows), weight_term)
    token_grad, weight_terms = lax.map(one_sample, (tokens, cotangent))
    weight_grad = lax.optimization_barrier(jnp.sum(weight_terms, axis=0)) / (N_REP * N_TY * N_TX)
    return (token_grad, weight_grad)
```

```python
import functools

import jax
import jax.numpy as jnp
import numpy as np
from jax import lax
from jax.experimental import pallas as pl
from jax.experimental.pallas import tpu as pltpu
from jax.sharding import PartitionSpec as P

HEADS = 16
HEAD_DIM = 32
GRID = 8
EPS = 1e-05
LANES = 128
BLOCK_HEADS = LANES // HEAD_DIM

BF16 = jnp.bfloat16
F32 = jnp.float32


def matmul(a, b, contract):
    return lax.dot_general(a, b, ((contract[:1], contract[1:]), ((), ())), preferred_element_type=F32)


def window_kernel(
    split_reps,
    pos_ref,
    pixels_ref,
    weight_ref,
    grad_ref,
    *refs,
):
    if split_reps:
        keep_ref, send_ref = refs[:2]
        refs = refs[2:]
    else:
        term_ref = refs[0]
        refs = refs[1:]
    normed_ref, standard_ref, cot_ref, query_ref, key_ref, value_ref, proj_ref = refs
    count, channels = cot_ref.shape
    win_tokens = GRID * GRID
    scale = HEAD_DIM**-0.5

    rows = lax.broadcasted_iota(jnp.int32, (count, count), 0)
    onehot = jnp.where(rows == pos_ref[...], 1.0, 0.0).astype(BF16)
    cot_ref[...] = matmul(onehot, pixels_ref[:, channels:], (1, 0)).astype(BF16)
    wide = matmul(onehot, pixels_ref[:, :channels], (1, 0))

    center = wide - jnp.mean(wide, axis=-1, keepdims=True)
    inv_std = lax.rsqrt(jnp.mean(center * center, axis=-1, keepdims=True) + EPS)
    standard = center * inv_std
    standard_ref[...] = standard
    normed = standard.astype(BF16)
    normed_ref[...] = normed

    query_ref[...] = (matmul(normed, weight_ref[:, :channels], (1, 0)) * scale).astype(BF16)
    key_ref[...] = matmul(normed, weight_ref[:, channels : 2 * channels], (1, 0)).astype(BF16)
    value_ref[...] = matmul(normed, weight_ref[:, 2 * channels :], (1, 0)).astype(BF16)

    stack_shape = (BLOCK_HEADS * win_tokens, LANES)
    own = lax.broadcasted_iota(jnp.int32, stack_shape, 0) // win_tokens == (
        lax.broadcasted_iota(jnp.int32, stack_shape, 1) // HEAD_DIM
    )
    mask = jnp.where(own, 1.0, 0.0)
    mask_low = mask.astype(BF16)

    def stack(block):
        return jnp.concatenate([block] * BLOCK_HEADS, axis=0) * mask_low

    for window in range(count // win_tokens):
        row = slice(window * win_tokens, (window + 1) * win_tokens)
        for block in range(channels // LANES):
            col = slice(block * LANES, (block + 1) * LANES)
            key = key_ref[row, col]
            queries = stack(query_ref[row, col])
            cots = stack(cot_ref[row, col])
            scores = matmul(key, queries, (1, 1))
            attn_grad = matmul(value_ref[row, col], cots, (1, 1))
            exponent = jnp.exp(scores - jnp.max(scores, axis=0, keepdims=True))
            probs = exponent * (1.0 / jnp.sum(exponent, axis=0, keepdims=True))
            score_grad = (
                probs * (attn_grad - jnp.sum(probs * attn_grad, axis=0, keepdims=True))
            ).astype(BF16)
            value_grad = matmul(probs.astype(BF16), cots, (1, 0))
            key_grad = matmul(score_grad, queries, (1, 0))
            spread = matmul(score_grad, key, (0, 0)) * mask
            query_grad = spread[:win_tokens]
            for head in range(1, BLOCK_HEADS):
                query_grad += spread[head * win_tokens : (head + 1) * win_tokens]
            base = block * LANES
            proj_ref[row, base : base + LANES] = (query_grad * scale).astype(BF16)
            base += channels
            proj_ref[row, base : base + LANES] = key_grad.astype(BF16)
            base += channels
            proj_ref[row, base : base + LANES] = value_grad.astype(BF16)

    if split_reps:
        half = 3 * channels // 2
        rep = lax.axis_index("rep")
        for ref, side in ((send_ref, 1 - rep), (keep_ref, rep)):
            start = pl.multiple_of(side * half, LANES)
            ref[...] = matmul(normed_ref[...], proj_ref[:, pl.ds(start, half)], (0, 0)).astype(BF16)
    else:
        term_ref[...] = matmul(normed_ref[...], proj_ref[...], (0, 0))

    normed_grad = matmul(proj_ref[...], weight_ref[...], (1, 1))
    standard = standard_ref[...]
    inner = (
        normed_grad
        - jnp.mean(normed_grad, axis=-1, keepdims=True)
        - standard * jnp.mean(normed_grad * standard, axis=-1, keepdims=True)
    )
    token_grad = (cot_ref[...].astype(F32) + inv_std * inner).astype(BF16)
    grad_ref[...] = matmul(onehot, token_grad, (0, 0)).astype(BF16)


def window_call(pos, pixels, weight, split_reps):
    count, channels = pixels.shape[0], pixels.shape[1] // 2
    vmem = pl.BlockSpec(memory_space=pltpu.VMEM)
    outs = [jax.ShapeDtypeStruct((count, channels), BF16)]
    if split_reps:
        outs += [jax.ShapeDtypeStruct((channels, 3 * channels // 2), BF16)] * 2
    else:
        outs += [jax.ShapeDtypeStruct((channels, 3 * channels), F32)]
    flat = (count, channels)
    return pl.pallas_call(
        functools.partial(window_kernel, split_reps),
        out_shape=outs,
        in_specs=[vmem] * 3,
        out_specs=[vmem] * len(outs),
        scratch_shapes=[
            pltpu.VMEM(flat, BF16),
            pltpu.VMEM(flat, F32),
            pltpu.VMEM(flat, BF16),
            pltpu.VMEM(flat, BF16),
            pltpu.VMEM(flat, BF16),
            pltpu.VMEM(flat, BF16),
            pltpu.VMEM((count, 3 * channels), BF16),
        ],
        compiler_params=pltpu.CompilerParams(vmem_limit_bytes=32 * 2**20),
        name="window_grads",
    )(pos, pixels, weight)


def swap_reps(values):
    return lax.ppermute(values, "rep", [(0, 1), (1, 0)])


def reduce_over(values, axis):
    size = lax.axis_size(axis)
    parts = values.reshape(size, values.shape[0] // size, *values.shape[1:])
    parts = lax.all_to_all(parts, axis, split_axis=0, concat_axis=0, tiled=True)
    return jnp.sum(parts.astype(F32), axis=0)


def shards(tokens, qkv_weight, cotangent):
    rep_count = lax.axis_size("rep")
    row_tiles = lax.axis_size("ty")
    col_tiles = lax.axis_size("tx")
    tile_count = row_tiles * col_tiles
    _, tile_height, tile_width, channels = tokens.shape
    stride_rows = row_tiles * tile_height // GRID
    stride_cols = col_tiles * tile_width // GRID
    block_rows = min(tile_height, stride_rows)
    fold_rows = stride_rows // block_rows
    col_groups = tile_width // stride_cols
    outer_rows = tile_height // block_rows
    inner_rows = block_rows // tile_count
    chunk = outer_rows * inner_rows * tile_width
    count = tile_count * chunk

    order = np.arange(count).reshape(
        row_tiles // fold_rows, fold_rows, col_tiles, outer_rows, inner_rows, col_groups, stride_cols
    )
    order = order.transpose(1, 4, 6, 0, 3, 2, 5).reshape(count)
    pos = np.zeros((1, count), np.int32)
    pos[0, order] = np.arange(count)

    def to_send(values):
        values = values.reshape(outer_rows, tile_count, inner_rows * tile_width, channels)
        return values.transpose(1, 0, 2, 3).reshape(tile_count, chunk, channels)

    sent = jnp.concatenate([to_send(tokens), to_send(cotangent)], axis=-1)
    pixels = lax.all_to_all(sent, ("ty", "tx"), split_axis=0, concat_axis=0, tiled=True)
    pixels = pixels.reshape(count, 2 * channels)
    split_reps = rep_count == 2
    outs = window_call(jnp.asarray(pos), pixels, qkv_weight, split_reps)
    spread = outs[0].reshape(tile_count, chunk, channels)

    total = rep_count * tile_count
    if split_reps:
        keep, send = outs[1:]
        half = keep.astype(F32) + swap_reps(send).astype(F32)
        half = half.astype(BF16).reshape(row_tiles, col_tiles, channels // tile_count, -1)
        rows = half.transpose(1, 0, 2, 3).reshape(channels, -1)
        rows = reduce_over(rows, "tx").astype(BF16)
        rows = reduce_over(rows, "ty") / total
        other = swap_reps(rows)
        first = lax.axis_index("rep") == 0
        weight_grad = jnp.concatenate(
            [jnp.where(first, rows, other), jnp.where(first, other, rows)], axis=1
        )
    else:
        weight_grad = lax.psum_scatter(outs[1], ("ty", "tx"), scatter_dimension=0, tiled=True)
        weight_grad = lax.psum(weight_grad, "rep") / total

    returned = lax.all_to_all(spread, ("ty", "tx"), split_axis=0, concat_axis=0, tiled=True)
    returned = returned.reshape(tile_count, outer_rows, inner_rows * tile_width, channels)
    token_grad = returned.transpose(1, 0, 2, 3).reshape(1, tile_height, tile_width, channels)
    return (token_grad, weight_grad)


def solution(mesh):
    placed = (P("rep", "ty", "tx", None), P(), P("rep", "ty", "tx", None))
    return jax.shard_map(
        shards,
        mesh=mesh,
        in_specs=placed,
        out_specs=(P("rep", "ty", "tx", None), P(("ty", "tx"), None)),
        check_vma=False,
    )
```

```python
import functools

import jax
import jax.numpy as jnp
import numpy as np
from jax import lax
from jax.experimental import pallas as pl
from jax.experimental.pallas import tpu as pltpu
from jax.sharding import PartitionSpec as P

HEADS = 16
HEAD_DIM = 32
GRID = 8
EPS = 1e-05
LANES = 128
BLOCK_HEADS = LANES // HEAD_DIM

BF16 = jnp.bfloat16
F32 = jnp.float32


def matmul(a, b, contract):
    return lax.dot_general(a, b, ((contract[:1], contract[1:]), ((), ())), preferred_element_type=F32)


def window_kernel(
    split_reps,
    pos_ref,
    pixels_ref,
    weight_ref,
    grad_ref,
    *refs,
):
    if split_reps:
        keep_ref, send_ref = refs[:2]
        refs = refs[2:]
    else:
        term_ref = refs[0]
        refs = refs[1:]
    normed_ref, standard_ref, cot_ref, query_ref, key_ref, value_ref, proj_ref = refs
    count, channels = cot_ref.shape
    win_tokens = GRID * GRID
    scale = HEAD_DIM**-0.5

    rows = lax.broadcasted_iota(jnp.int32, (count, count), 0)
    onehot = jnp.where(rows == pos_ref[...], 1.0, 0.0).astype(BF16)
    cot_ref[...] = matmul(onehot, pixels_ref[:, channels:], (1, 0)).astype(BF16)
    wide = matmul(onehot, pixels_ref[:, :channels], (1, 0))

    center = wide - jnp.mean(wide, axis=-1, keepdims=True)
    inv_std = lax.rsqrt(jnp.mean(center * center, axis=-1, keepdims=True) + EPS)
    standard = center * inv_std
    standard_ref[...] = standard
    normed = standard.astype(BF16)
    normed_ref[...] = normed

    query_ref[...] = (matmul(normed, weight_ref[:, :channels], (1, 0)) * scale).astype(BF16)
    key_ref[...] = matmul(normed, weight_ref[:, channels : 2 * channels], (1, 0)).astype(BF16)
    value_ref[...] = matmul(normed, weight_ref[:, 2 * channels :], (1, 0)).astype(BF16)

    stack_shape = (BLOCK_HEADS * win_tokens, LANES)
    own = lax.broadcasted_iota(jnp.int32, stack_shape, 0) // win_tokens == (
        lax.broadcasted_iota(jnp.int32, stack_shape, 1) // HEAD_DIM
    )
    mask = jnp.where(own, 1.0, 0.0)
    mask_low = mask.astype(BF16)

    def stack(block):
        return jnp.concatenate([block] * BLOCK_HEADS, axis=0) * mask_low

    for window in range(count // win_tokens):
        row = slice(window * win_tokens, (window + 1) * win_tokens)
        for block in range(channels // LANES):
            col = slice(block * LANES, (block + 1) * LANES)
            key = key_ref[row, col]
            queries = stack(query_ref[row, col])
            cots = stack(cot_ref[row, col])
            scores = matmul(key, queries, (1, 1))
            attn_grad = matmul(value_ref[row, col], cots, (1, 1))
            exponent = jnp.exp(scores - jnp.max(scores, axis=0, keepdims=True))
            probs = exponent * (1.0 / jnp.sum(exponent, axis=0, keepdims=True))
            score_grad = (
                probs * (attn_grad - jnp.sum(probs * attn_grad, axis=0, keepdims=True))
            ).astype(BF16)
            value_grad = matmul(probs.astype(BF16), cots, (1, 0))
            key_grad = matmul(score_grad, queries, (1, 0))
            spread = matmul(score_grad, key, (0, 0)) * mask
            query_grad = spread[:win_tokens]
            for head in range(1, BLOCK_HEADS):
                query_grad += spread[head * win_tokens : (head + 1) * win_tokens]
            base = block * LANES
            proj_ref[row, base : base + LANES] = (query_grad * scale).astype(BF16)
            base += channels
            proj_ref[row, base : base + LANES] = key_grad.astype(BF16)
            base += channels
            proj_ref[row, base : base + LANES] = value_grad.astype(BF16)

    if split_reps:
        half = 3 * channels // 2
        rep = lax.axis_index("rep")
        for ref, side in ((send_ref, 1 - rep), (keep_ref, rep)):
            start = pl.multiple_of(side * half, LANES)
            ref[...] = matmul(normed_ref[...], proj_ref[:, pl.ds(start, half)], (0, 0)).astype(BF16)
    else:
        term_ref[...] = matmul(normed_ref[...], proj_ref[...], (0, 0))

    normed_grad = matmul(proj_ref[...], weight_ref[...], (1, 1))
    standard = standard_ref[...]
    inner = (
        normed_grad
        - jnp.mean(normed_grad, axis=-1, keepdims=True)
        - standard * jnp.mean(normed_grad * standard, axis=-1, keepdims=True)
    )
    token_grad = (cot_ref[...].astype(F32) + inv_std * inner).astype(BF16)
    grad_ref[...] = matmul(onehot, token_grad, (0, 0)).astype(BF16)


def window_call(pos, pixels, weight, split_reps):
    count, channels = pixels.shape[0], pixels.shape[1] // 2
    vmem = pl.BlockSpec(memory_space=pltpu.VMEM)
    outs = [jax.ShapeDtypeStruct((count, channels), BF16)]
    if split_reps:
        outs += [jax.ShapeDtypeStruct((channels, 3 * channels // 2), BF16)] * 2
    else:
        outs += [jax.ShapeDtypeStruct((channels, 3 * channels), F32)]
    flat = (count, channels)
    return pl.pallas_call(
        functools.partial(window_kernel, split_reps),
        out_shape=outs,
        in_specs=[vmem] * 3,
        out_specs=[vmem] * len(outs),
        scratch_shapes=[
            pltpu.VMEM(flat, BF16),
            pltpu.VMEM(flat, F32),
            pltpu.VMEM(flat, BF16),
            pltpu.VMEM(flat, BF16),
            pltpu.VMEM(flat, BF16),
            pltpu.VMEM(flat, BF16),
            pltpu.VMEM((count, 3 * channels), BF16),
        ],
        compiler_params=pltpu.CompilerParams(vmem_limit_bytes=32 * 2**20),
        name="window_grads",
    )(pos, pixels, weight)


def swap_reps(values):
    return lax.ppermute(values, "rep", [(0, 1), (1, 0)])


def reduce_over(parts, axis, dim):
    size = lax.axis_size(axis)
    me = lax.axis_index(axis)
    total = lax.dynamic_index_in_dim(parts, me, dim, keepdims=False).astype(F32)
    for step in range(1, size):
        part = lax.dynamic_index_in_dim(parts, me ^ step, dim, keepdims=False)
        total += lax.ppermute(part, axis, [(i, i ^ step) for i in range(size)]).astype(F32)
    return total


def shards(tokens, qkv_weight, cotangent):
    rep_count = lax.axis_size("rep")
    row_tiles = lax.axis_size("ty")
    col_tiles = lax.axis_size("tx")
    tile_count = row_tiles * col_tiles
    _, tile_height, tile_width, channels = tokens.shape
    stride_rows = row_tiles * tile_height // GRID
    stride_cols = col_tiles * tile_width // GRID
    block_rows = min(tile_height, stride_rows)
    fold_rows = stride_rows // block_rows
    col_groups = tile_width // stride_cols
    outer_rows = tile_height // block_rows
    inner_rows = block_rows // tile_count
    chunk = outer_rows * inner_rows * tile_width
    count = tile_count * chunk

    order = np.arange(count).reshape(
        row_tiles // fold_rows, fold_rows, col_tiles, outer_rows, inner_rows, col_groups, stride_cols
    )
    order = order.transpose(1, 4, 6, 0, 3, 2, 5).reshape(count)
    pos = np.zeros((1, count), np.int32)
    pos[0, order] = np.arange(count)

    def to_send(values):
        values = values.reshape(outer_rows, tile_count, inner_rows * tile_width, channels)
        return values.transpose(1, 0, 2, 3).reshape(tile_count, chunk, channels)

    sent = jnp.concatenate([to_send(tokens), to_send(cotangent)], axis=-1)
    pixels = lax.all_to_all(sent, ("ty", "tx"), split_axis=0, concat_axis=0, tiled=True)
    pixels = pixels.reshape(count, 2 * channels)
    split_reps = rep_count == 2
    outs = window_call(jnp.asarray(pos), pixels, qkv_weight, split_reps)
    spread = outs[0].reshape(tile_count, chunk, channels)
    returned = lax.all_to_all(spread, ("ty", "tx"), split_axis=0, concat_axis=0, tiled=True)

    total = rep_count * tile_count
    if split_reps:
        keep, send = outs[1:]
        half = keep.astype(F32) + swap_reps(send).astype(F32)
        half = half.astype(BF16).reshape(row_tiles, col_tiles, channels // tile_count, -1)
        rows = reduce_over(half, "tx", 1).astype(BF16)
        rows, returned = lax.optimization_barrier((rows, returned))
        rows = reduce_over(rows, "ty", 0) / total
        other = swap_reps(rows)
        first = lax.axis_index("rep") == 0
        weight_grad = jnp.concatenate(
            [jnp.where(first, rows, other), jnp.where(first, other, rows)], axis=1
        )
    else:
        weight_grad = lax.psum_scatter(outs[1], ("ty", "tx"), scatter_dimension=0, tiled=True)
        weight_grad = lax.psum(weight_grad, "rep") / total

    returned = returned.reshape(tile_count, outer_rows, inner_rows * tile_width, channels)
    token_grad = returned.transpose(1, 0, 2, 3).reshape(1, tile_height, tile_width, channels)
    return (token_grad, weight_grad)


def solution(mesh):
    placed = (P("rep", "ty", "tx", None), P(), P("rep", "ty", "tx", None))
    return jax.shard_map(
        shards,
        mesh=mesh,
        in_specs=placed,
        out_specs=(P("rep", "ty", "tx", None), P(("ty", "tx"), None)),
        check_vma=False,
    )
```

```python
import functools

import jax
import jax.numpy as jnp
import numpy as np
from jax import lax
from jax.experimental import pallas as pl
from jax.experimental.pallas import tpu as pltpu
from jax.sharding import PartitionSpec as P

HEADS = 16
HEAD_DIM = 32
GRID = 8
EPS = 1e-05
LANES = 128
BLOCK_HEADS = LANES // HEAD_DIM
GROUP = 8

BF16 = jnp.bfloat16
F32 = jnp.float32


def matmul(a, b, contract):
    return lax.dot_general(a, b, ((contract[:1], contract[1:]), ((), ())), preferred_element_type=F32)


def window_kernel(
    split_reps,
    pos_ref,
    pixels_ref,
    weight_ref,
    grad_ref,
    *refs,
):
    if split_reps:
        keep_ref, send_ref = refs[:2]
        refs = refs[2:]
    else:
        term_ref = refs[0]
        refs = refs[1:]
    normed_ref, standard_ref, cot_ref, query_ref, key_ref, value_ref, proj_ref = refs
    count, channels = cot_ref.shape
    win_tokens = GRID * GRID
    scale = HEAD_DIM**-0.5

    rows = lax.broadcasted_iota(jnp.int32, (count, count), 0)
    onehot = jnp.where(rows == pos_ref[...], 1.0, 0.0).astype(BF16)
    cot_ref[...] = matmul(onehot, pixels_ref[:, channels:], (1, 0)).astype(BF16)
    wide = matmul(onehot, pixels_ref[:, :channels], (1, 0))

    center = wide - jnp.mean(wide, axis=-1, keepdims=True)
    inv_std = lax.rsqrt(jnp.mean(center * center, axis=-1, keepdims=True) + EPS)
    standard = center * inv_std
    standard_ref[...] = standard
    normed = standard.astype(BF16)
    normed_ref[...] = normed

    query_ref[...] = (matmul(normed, weight_ref[:, :channels], (1, 0)) * scale).astype(BF16)
    key_ref[...] = matmul(normed, weight_ref[:, channels : 2 * channels], (1, 0)).astype(BF16)
    value_ref[...] = matmul(normed, weight_ref[:, 2 * channels :], (1, 0)).astype(BF16)

    stack_shape = (BLOCK_HEADS * win_tokens, LANES)
    own = lax.broadcasted_iota(jnp.int32, stack_shape, 0) // win_tokens == (
        lax.broadcasted_iota(jnp.int32, stack_shape, 1) // HEAD_DIM
    )
    mask = jnp.where(own, 1.0, 0.0)
    mask_low = mask.astype(BF16)

    def stack(block):
        return jnp.concatenate([block] * BLOCK_HEADS, axis=0) * mask_low

    cells = [
        (slice(row, row + win_tokens), slice(col, col + LANES))
        for row in range(0, count, win_tokens)
        for col in range(0, channels, LANES)
    ]
    for first in range(0, len(cells), GROUP):
        group = cells[first : first + GROUP]
        raw = []
        for row, col in group:
            scores = matmul(key_ref[row, col], stack(query_ref[row, col]), (1, 1))
            attn_grad = matmul(value_ref[row, col], stack(cot_ref[row, col]), (1, 1))
            raw.append((scores, attn_grad))
        low = []
        for scores, attn_grad in raw:
            exponent = jnp.exp(scores - jnp.max(scores, axis=0, keepdims=True))
            probs = exponent * (1.0 / jnp.sum(exponent, axis=0, keepdims=True))
            score_grad = probs * (attn_grad - jnp.sum(probs * attn_grad, axis=0, keepdims=True))
            low.append((probs.astype(BF16), score_grad.astype(BF16)))
        for (row, col), (probs, score_grad) in zip(group, low):
            value_grad = matmul(probs, stack(cot_ref[row, col]), (1, 0))
            key_grad = matmul(score_grad, stack(query_ref[row, col]), (1, 0))
            spread = matmul(score_grad, key_ref[row, col], (0, 0)) * mask
            query_grad = spread[:win_tokens]
            for head in range(1, BLOCK_HEADS):
                query_grad += spread[head * win_tokens : (head + 1) * win_tokens]
            for part, grad in enumerate((query_grad * scale, key_grad, value_grad)):
                base = part * channels + col.start
                proj_ref[row, base : base + LANES] = grad.astype(BF16)

    if split_reps:
        half = 3 * channels // 2
        rep = lax.axis_index("rep")
        for ref, side in ((send_ref, 1 - rep), (keep_ref, rep)):
            start = pl.multiple_of(side * half, LANES)
            ref[...] = matmul(normed_ref[...], proj_ref[:, pl.ds(start, half)], (0, 0)).astype(BF16)
    else:
        term_ref[...] = matmul(normed_ref[...], proj_ref[...], (0, 0))

    normed_grad = matmul(proj_ref[...], weight_ref[...], (1, 1))
    standard = standard_ref[...]
    inner = (
        normed_grad
        - jnp.mean(normed_grad, axis=-1, keepdims=True)
        - standard * jnp.mean(normed_grad * standard, axis=-1, keepdims=True)
    )
    token_grad = (cot_ref[...].astype(F32) + inv_std * inner).astype(BF16)
    grad_ref[...] = matmul(onehot, token_grad, (0, 0)).astype(BF16)


def window_call(pos, pixels, weight, split_reps):
    count, channels = pixels.shape[0], pixels.shape[1] // 2
    vmem = pl.BlockSpec(memory_space=pltpu.VMEM)
    outs = [jax.ShapeDtypeStruct((count, channels), BF16)]
    if split_reps:
        outs += [jax.ShapeDtypeStruct((channels, 3 * channels // 2), BF16)] * 2
    else:
        outs += [jax.ShapeDtypeStruct((channels, 3 * channels), F32)]
    flat = (count, channels)
    return pl.pallas_call(
        functools.partial(window_kernel, split_reps),
        out_shape=outs,
        in_specs=[vmem] * 3,
        out_specs=[vmem] * len(outs),
        scratch_shapes=[
            pltpu.VMEM(flat, BF16),
            pltpu.VMEM(flat, F32),
            pltpu.VMEM(flat, BF16),
            pltpu.VMEM(flat, BF16),
            pltpu.VMEM(flat, BF16),
            pltpu.VMEM(flat, BF16),
            pltpu.VMEM((count, 3 * channels), BF16),
        ],
        compiler_params=pltpu.CompilerParams(vmem_limit_bytes=32 * 2**20),
        name="window_grads",
    )(pos, pixels, weight)


def swap_reps(values):
    return lax.ppermute(values, "rep", [(0, 1), (1, 0)])


def reduce_over(parts, axis, dim):
    size = lax.axis_size(axis)
    me = lax.axis_index(axis)
    total = lax.dynamic_index_in_dim(parts, me, dim, keepdims=False).astype(F32)
    for step in range(1, size):
        part = lax.dynamic_index_in_dim(parts, me ^ step, dim, keepdims=False)
        total += lax.ppermute(part, axis, [(i, i ^ step) for i in range(size)]).astype(F32)
    return total


def shards(tokens, qkv_weight, cotangent):
    rep_count = lax.axis_size("rep")
    row_tiles = lax.axis_size("ty")
    col_tiles = lax.axis_size("tx")
    tile_count = row_tiles * col_tiles
    _, tile_height, tile_width, channels = tokens.shape
    stride_rows = row_tiles * tile_height // GRID
    stride_cols = col_tiles * tile_width // GRID
    block_rows = min(tile_height, stride_rows)
    fold_rows = stride_rows // block_rows
    col_groups = tile_width // stride_cols
    outer_rows = tile_height // block_rows
    inner_rows = block_rows // tile_count
    chunk = outer_rows * inner_rows * tile_width
    count = tile_count * chunk

    order = np.arange(count).reshape(
        row_tiles // fold_rows, fold_rows, col_tiles, outer_rows, inner_rows, col_groups, stride_cols
    )
    order = order.transpose(1, 4, 6, 0, 3, 2, 5).reshape(count)
    pos = np.zeros((1, count), np.int32)
    pos[0, order] = np.arange(count)

    def to_send(values):
        values = values.reshape(outer_rows, tile_count, inner_rows * tile_width, channels)
        return values.transpose(1, 0, 2, 3).reshape(tile_count, chunk, channels)

    sent = jnp.concatenate([to_send(tokens), to_send(cotangent)], axis=-1)
    pixels = lax.all_to_all(sent, ("ty", "tx"), split_axis=0, concat_axis=0, tiled=True)
    pixels = pixels.reshape(count, 2 * channels)
    split_reps = rep_count == 2
    outs = window_call(jnp.asarray(pos), pixels, qkv_weight, split_reps)
    spread = outs[0].reshape(tile_count, chunk, channels)
    returned = lax.all_to_all(spread, ("ty", "tx"), split_axis=0, concat_axis=0, tiled=True)

    total = rep_count * tile_count
    if split_reps:
        keep, send = outs[1:]
        half = keep.astype(F32) + swap_reps(send).astype(F32)
        half = half.astype(BF16).reshape(row_tiles, col_tiles, channels // tile_count, -1)
        rows = reduce_over(half, "tx", 1).astype(BF16)
        rows = reduce_over(rows, "ty", 0) / total
        other = swap_reps(rows)
        first = lax.axis_index("rep") == 0
        weight_grad = jnp.concatenate(
            [jnp.where(first, rows, other), jnp.where(first, other, rows)], axis=1
        )
    else:
        weight_grad = lax.psum_scatter(outs[1], ("ty", "tx"), scatter_dimension=0, tiled=True)
        weight_grad = lax.psum(weight_grad, "rep") / total

    returned = returned.reshape(tile_count, outer_rows, inner_rows * tile_width, channels)
    token_grad = returned.transpose(1, 0, 2, 3).reshape(1, tile_height, tile_width, channels)
    return (token_grad, weight_grad)


def solution(mesh):
    placed = (P("rep", "ty", "tx", None), P(), P("rep", "ty", "tx", None))
    return jax.shard_map(
        shards,
        mesh=mesh,
        in_specs=placed,
        out_specs=(P("rep", "ty", "tx", None), P(("ty", "tx"), None)),
        check_vma=False,
    )
```

```python
import functools

import jax
import jax.numpy as jnp
import numpy as np
from jax import lax
from jax.experimental import pallas as pl
from jax.experimental.pallas import tpu as pltpu
from jax.sharding import PartitionSpec as P

HEADS = 16
HEAD_DIM = 32
GRID = 8
EPS = 1e-05
LANES = 128
BLOCK_HEADS = LANES // HEAD_DIM
GROUP = 8

BF16 = jnp.bfloat16
F32 = jnp.float32


def matmul(a, b, contract):
    return lax.dot_general(a, b, ((contract[:1], contract[1:]), ((), ())), preferred_element_type=F32)


def normalize(pixels):
    center = pixels - jnp.mean(pixels, axis=-1, keepdims=True)
    inv_std = lax.rsqrt(jnp.mean(center * center, axis=-1, keepdims=True) + EPS)
    return center * inv_std, inv_std


def vmem_call(kernel, outs, name, *args, scratch=(), mib=8, remote=()):
    vmem = pl.BlockSpec(memory_space=pltpu.VMEM)
    hbm = pl.BlockSpec(memory_space=pltpu.HBM)
    return pl.pallas_call(
        kernel,
        out_shape=outs,
        in_specs=[hbm if index in remote else vmem for index in range(len(args))],
        out_specs=[vmem] * len(outs),
        scratch_shapes=scratch,
        compiler_params=pltpu.CompilerParams(vmem_limit_bytes=mib * 2**20),
        name=name,
    )(*args)


def pack_kernel(shape, tokens_ref, cot_ref, sent_ref, tokens_buf, cot_buf, sems):
    outer, tiles, size = shape
    channels = sent_ref.shape[2] // 2
    height = tokens_buf.shape[0] // outer
    copies = []
    for index in range(outer):
        rows = pl.ds(index * height, height)
        for part, (ref, buf) in enumerate(((tokens_ref, tokens_buf), (cot_ref, cot_buf))):
            copy = pltpu.make_async_copy(ref.at[rows], buf.at[rows], sems.at[part, index])
            copy.start()
            copies.append(copy)
    for index in range(outer):
        rows = slice(index * height, (index + 1) * height)
        out = slice(index * size, (index + 1) * size)
        copies[2 * index].wait()
        pixels = tokens_buf[rows].reshape(tiles * size, channels).astype(F32)
        normed = normalize(pixels)[0].astype(BF16)
        sent_ref[:, out, :channels] = normed.reshape(tiles, size, channels)
        copies[2 * index + 1].wait()
        sent_ref[:, out, channels:] = cot_buf[rows].reshape(tiles, size, channels)


def unpack_kernel(shape, returned_ref, tokens_ref, cot_ref, grad_ref):
    height, width, channels = tokens_ref.shape
    outer, _, size = shape
    flat = (height * width, channels)
    standard, inv_std = normalize(tokens_ref[...].reshape(flat).astype(F32))
    normed_grad = jnp.concatenate(
        [
            returned_ref[:, index * size : (index + 1) * size].reshape(-1, channels)
            for index in range(outer)
        ],
        axis=0,
    ).astype(F32)
    inner = (
        normed_grad
        - jnp.mean(normed_grad, axis=-1, keepdims=True)
        - standard * jnp.mean(normed_grad * standard, axis=-1, keepdims=True)
    )
    token_grad = cot_ref[...].reshape(flat).astype(F32) + inv_std * inner
    grad_ref[...] = token_grad.astype(BF16).reshape(height, width, channels)


def window_order(pos_ref):
    count = pos_ref.shape[1]
    rows = lax.broadcasted_iota(jnp.int32, (count, count), 0)
    return jnp.where(rows == pos_ref[...], 1.0, 0.0).astype(BF16)


def weight_term(normed_ref, proj_ref, side):
    half = proj_ref.shape[1] // 2
    start = pl.multiple_of(side * half, LANES)
    return matmul(normed_ref[...], proj_ref[:, pl.ds(start, half)], (0, 0))


def window_kernel(
    split_reps,
    pos_ref,
    pixels_ref,
    weight_ref,
    proj_ref,
    normed_ref,
    term_ref,
    cot_ref,
    query_ref,
    key_ref,
    value_ref,
):
    count, channels = cot_ref.shape
    win_tokens = GRID * GRID
    scale = HEAD_DIM**-0.5

    onehot = window_order(pos_ref)
    normed = matmul(onehot, pixels_ref[:, :channels], (1, 0)).astype(BF16)
    normed_ref[...] = normed
    cot_ref[...] = matmul(onehot, pixels_ref[:, channels:], (1, 0)).astype(BF16)

    query_ref[...] = (matmul(normed, weight_ref[:, :channels], (1, 0)) * scale).astype(BF16)
    key_ref[...] = matmul(normed, weight_ref[:, channels : 2 * channels], (1, 0)).astype(BF16)
    value_ref[...] = matmul(normed, weight_ref[:, 2 * channels :], (1, 0)).astype(BF16)

    stack_shape = (BLOCK_HEADS * win_tokens, LANES)
    own = lax.broadcasted_iota(jnp.int32, stack_shape, 0) // win_tokens == (
        lax.broadcasted_iota(jnp.int32, stack_shape, 1) // HEAD_DIM
    )
    mask = jnp.where(own, 1.0, 0.0)
    mask_low = mask.astype(BF16)

    def stack(block):
        return jnp.concatenate([block] * BLOCK_HEADS, axis=0) * mask_low

    cells = [
        (slice(row, row + win_tokens), slice(col, col + LANES))
        for row in range(0, count, win_tokens)
        for col in range(0, channels, LANES)
    ]
    for first in range(0, len(cells), GROUP):
        group = cells[first : first + GROUP]
        raw = []
        for row, col in group:
            scores = matmul(key_ref[row, col], stack(query_ref[row, col]), (1, 1))
            attn_grad = matmul(value_ref[row, col], stack(cot_ref[row, col]), (1, 1))
            raw.append((scores, attn_grad))
        low = []
        for scores, attn_grad in raw:
            exponent = jnp.exp(scores - jnp.max(scores, axis=0, keepdims=True))
            probs = exponent * (1.0 / jnp.sum(exponent, axis=0, keepdims=True))
            score_grad = probs * (attn_grad - jnp.sum(probs * attn_grad, axis=0, keepdims=True))
            low.append((probs.astype(BF16), score_grad.astype(BF16)))
        for (row, col), (probs, score_grad) in zip(group, low):
            value_grad = matmul(probs, stack(cot_ref[row, col]), (1, 0))
            key_grad = matmul(score_grad, stack(query_ref[row, col]), (1, 0))
            spread = matmul(score_grad, key_ref[row, col], (0, 0)) * mask
            query_grad = spread[:win_tokens]
            for head in range(1, BLOCK_HEADS):
                query_grad += spread[head * win_tokens : (head + 1) * win_tokens]
            for part, grad in enumerate((query_grad * scale, key_grad, value_grad)):
                base = part * channels + col.start
                proj_ref[row, base : base + LANES] = grad.astype(BF16)

    if split_reps:
        term_ref[...] = weight_term(normed_ref, proj_ref, 1 - lax.axis_index("rep")).astype(BF16)
    else:
        term_ref[...] = matmul(normed_ref[...], proj_ref[...], (0, 0))


def back_kernel(split_reps, pos_ref, proj_ref, normed_ref, weight_ref, grad_ref, *keep_refs):
    if split_reps:
        keep_refs[0][...] = weight_term(normed_ref, proj_ref, lax.axis_index("rep")).astype(BF16)
    normed_grad = matmul(proj_ref[...], weight_ref[...], (1, 1)).astype(BF16)
    grad_ref[...] = matmul(window_order(pos_ref), normed_grad, (0, 0)).astype(BF16)


def swap_reps(values):
    return lax.ppermute(values, "rep", [(0, 1), (1, 0)])


def split_kernel(axis, keep_ref, got_ref, *part_refs):
    me = lax.axis_index(axis)
    for step, ref in enumerate(part_refs):
        ref[...] = (keep_ref[:, me ^ step].astype(F32) + got_ref[:, me ^ step].astype(F32)).astype(BF16)


def exchange(parts, axis):
    size = len(parts)
    total = parts[0].astype(F32)
    for step in range(1, size):
        total += lax.ppermute(parts[step], axis, [(i, i ^ step) for i in range(size)]).astype(F32)
    return total


def reduce_over(parts, axis, dim):
    size = lax.axis_size(axis)
    me = lax.axis_index(axis)
    total = lax.dynamic_index_in_dim(parts, me, dim, keepdims=False).astype(F32)
    for step in reversed(range(1, size)):
        part = lax.dynamic_index_in_dim(parts, me ^ step, dim, keepdims=False)
        total += lax.ppermute(part, axis, [(i, i ^ step) for i in range(size)]).astype(F32)
    return total


def shards(tokens, qkv_weight, cotangent):
    rep_count = lax.axis_size("rep")
    row_tiles = lax.axis_size("ty")
    col_tiles = lax.axis_size("tx")
    tile_count = row_tiles * col_tiles
    _, tile_height, tile_width, channels = tokens.shape
    stride_rows = row_tiles * tile_height // GRID
    stride_cols = col_tiles * tile_width // GRID
    block_rows = min(tile_height, stride_rows)
    fold_rows = stride_rows // block_rows
    col_groups = tile_width // stride_cols
    outer_rows = tile_height // block_rows
    inner_rows = block_rows // tile_count
    chunk = outer_rows * inner_rows * tile_width
    count = tile_count * chunk

    order = np.arange(count).reshape(
        row_tiles // fold_rows, fold_rows, col_tiles, outer_rows, inner_rows, col_groups, stride_cols
    )
    order = order.transpose(1, 4, 6, 0, 3, 2, 5).reshape(count)
    pos = np.zeros((1, count), np.int32)
    pos[0, order] = np.arange(count)

    local = (tile_height, tile_width, channels)
    split_shape = (outer_rows, tile_count, inner_rows * tile_width)
    tokens, cotangent = tokens.reshape(local), cotangent.reshape(local)
    (sent,) = vmem_call(
        functools.partial(pack_kernel, split_shape),
        [jax.ShapeDtypeStruct((tile_count, chunk, 2 * channels), BF16)],
        "pack",
        pltpu.with_memory_space_constraint(tokens, pltpu.HBM),
        pltpu.with_memory_space_constraint(cotangent, pltpu.HBM),
        scratch=[
            pltpu.VMEM(local, BF16),
            pltpu.VMEM(local, BF16),
            pltpu.SemaphoreType.DMA((2, outer_rows)),
        ],
        remote=(0, 1),
    )
    pixels = lax.all_to_all(sent, ("ty", "tx"), split_axis=0, concat_axis=0, tiled=True)
    pixels = pixels.reshape(count, 2 * channels)

    split_reps = rep_count == 2
    flat = jax.ShapeDtypeStruct((count, channels), BF16)
    term = jax.ShapeDtypeStruct((channels, 3 * channels // 2), BF16)
    whole = jax.ShapeDtypeStruct((channels, 3 * channels), F32)
    proj_grad, normed, send = vmem_call(
        functools.partial(window_kernel, split_reps),
        [
            jax.ShapeDtypeStruct((count, 3 * channels), BF16),
            flat,
            term if split_reps else whole,
        ],
        "window_grads",
        jnp.asarray(pos),
        pixels,
        qkv_weight,
        scratch=[pltpu.VMEM((count, channels), BF16)] * 4,
        mib=16,
    )
    normed_grad, *keep = vmem_call(
        functools.partial(back_kernel, split_reps),
        [flat] + [term] * split_reps,
        "normed_grad",
        jnp.asarray(pos),
        proj_grad,
        normed,
        qkv_weight,
    )
    spread = normed_grad.reshape(tile_count, chunk, channels)
    returned = lax.all_to_all(spread, ("ty", "tx"), split_axis=0, concat_axis=0, tiled=True)

    total = rep_count * tile_count
    if split_reps:
        shape = (row_tiles, col_tiles, channels // tile_count, 3 * channels // 2)
        part = jax.ShapeDtypeStruct((shape[0], *shape[2:]), BF16)
        parts = vmem_call(
            functools.partial(split_kernel, "tx"),
            [part] * col_tiles,
            "split_tx",
            keep[0].reshape(shape),
            swap_reps(send).reshape(shape),
        )
        rows = exchange(parts, "tx").astype(BF16)
        rows = reduce_over(rows, "ty", 0) / total
        other = swap_reps(rows)
        first = lax.axis_index("rep") == 0
        weight_grad = jnp.concatenate(
            [jnp.where(first, rows, other), jnp.where(first, other, rows)], axis=1
        )
    else:
        weight_grad = lax.psum_scatter(send, ("ty", "tx"), scatter_dimension=0, tiled=True)
        weight_grad = lax.psum(weight_grad, "rep") / total

    (token_grad,) = vmem_call(
        functools.partial(unpack_kernel, split_shape),
        [jax.ShapeDtypeStruct(local, BF16)],
        "token_grad",
        returned,
        tokens,
        cotangent,
    )
    token_grad = token_grad.reshape(1, *local)
    return (token_grad, weight_grad)


def solution(mesh):
    placed = (P("rep", "ty", "tx", None), P(), P("rep", "ty", "tx", None))
    return jax.shard_map(
        shards,
        mesh=mesh,
        in_specs=placed,
        out_specs=(P("rep", "ty", "tx", None), P(("ty", "tx"), None)),
        check_vma=False,
    )
```

```python
import functools

import jax
import jax.numpy as jnp
import numpy as np
from jax import lax
from jax.experimental import pallas as pl
from jax.experimental.pallas import tpu as pltpu
from jax.sharding import PartitionSpec as P

HEADS = 16
HEAD_DIM = 32
GRID = 8
EPS = 1e-05
LANES = 128
BLOCK_HEADS = LANES // HEAD_DIM
GROUP = 8

BF16 = jnp.bfloat16
F32 = jnp.float32


def matmul(a, b, contract):
    return lax.dot_general(a, b, ((contract[:1], contract[1:]), ((), ())), preferred_element_type=F32)


def normalize(pixels):
    center = pixels - jnp.mean(pixels, axis=-1, keepdims=True)
    inv_std = lax.rsqrt(jnp.mean(center * center, axis=-1, keepdims=True) + EPS)
    return center * inv_std, inv_std


def vmem_call(kernel, outs, name, *args, scratch=(), mib=8, remote=()):
    vmem = pl.BlockSpec(memory_space=pltpu.VMEM)
    hbm = pl.BlockSpec(memory_space=pltpu.HBM)
    return pl.pallas_call(
        kernel,
        out_shape=outs,
        in_specs=[hbm if index in remote else vmem for index in range(len(args))],
        out_specs=[vmem] * len(outs),
        scratch_shapes=scratch,
        compiler_params=pltpu.CompilerParams(vmem_limit_bytes=mib * 2**20),
        name=name,
    )(*args)


def in_chunks(shape, pixels):
    channels = pixels.shape[-1]
    pixels = pixels.astype(F32).reshape(*shape, channels)
    return jnp.concatenate([pixels[index] for index in range(shape[0])], axis=1)


def pack_kernel(shape, tokens_ref, cot_ref, sent_ref, tokens_buf, cot_buf, sems):
    channels = tokens_buf.shape[2]
    copies = [
        pltpu.make_async_copy(tokens_ref, tokens_buf, sems.at[0]),
        pltpu.make_async_copy(cot_ref, cot_buf, sems.at[1]),
    ]
    for copy in copies:
        copy.start()
    copies[0].wait()
    sent_ref[:, :, :channels] = normalize(in_chunks(shape, tokens_buf[...]))[0].astype(BF16)
    copies[1].wait()
    sent_ref[:, :, channels:] = in_chunks(shape, cot_buf[...]).astype(BF16)


def unpack_kernel(shape, returned_ref, tokens_ref, cot_ref, grad_ref):
    outer, tiles, size = shape
    standard, inv_std = normalize(in_chunks(shape, tokens_ref[...]))
    normed_grad = returned_ref[...].astype(F32)
    inner = (
        normed_grad
        - jnp.mean(normed_grad, axis=-1, keepdims=True)
        - standard * jnp.mean(normed_grad * standard, axis=-1, keepdims=True)
    )
    grad = in_chunks(shape, cot_ref[...]) + inv_std * inner
    rows = grad_ref.shape[0] // outer
    for index in range(outer):
        part = grad[:, index * size : (index + 1) * size].astype(BF16)
        grad_ref[index * rows : (index + 1) * rows] = part.reshape(rows, *grad_ref.shape[1:])


def window_order(pos_ref):
    count = pos_ref.shape[1]
    rows = lax.broadcasted_iota(jnp.int32, (count, count), 0)
    return jnp.where(rows == pos_ref[...], 1.0, 0.0).astype(BF16)


def half_slices(halves, side, channels):
    width = channels // halves
    return [pl.ds(pl.multiple_of(part * channels + side * width, LANES), width) for part in range(3)]


def attend(weight_ref, columns, normed, scratch, proj_ref):
    cot_ref, query_ref, key_ref, value_ref = scratch
    count, width = cot_ref.shape
    win_tokens = GRID * GRID
    scale = HEAD_DIM**-0.5

    query_ref[...] = (matmul(normed, weight_ref[:, columns[0]], (1, 0)) * scale).astype(BF16)
    key_ref[...] = matmul(normed, weight_ref[:, columns[1]], (1, 0)).astype(BF16)
    value_ref[...] = matmul(normed, weight_ref[:, columns[2]], (1, 0)).astype(BF16)

    stack_shape = (BLOCK_HEADS * win_tokens, LANES)
    own = lax.broadcasted_iota(jnp.int32, stack_shape, 0) // win_tokens == (
        lax.broadcasted_iota(jnp.int32, stack_shape, 1) // HEAD_DIM
    )
    mask = jnp.where(own, 1.0, 0.0)
    mask_low = mask.astype(BF16)

    def stack(block):
        return jnp.concatenate([block] * BLOCK_HEADS, axis=0) * mask_low

    cells = [
        (slice(row, row + win_tokens), slice(col, col + LANES))
        for row in range(0, count, win_tokens)
        for col in range(0, width, LANES)
    ]
    for first in range(0, len(cells), GROUP):
        group = cells[first : first + GROUP]
        raw = []
        for row, col in group:
            scores = matmul(key_ref[row, col], stack(query_ref[row, col]), (1, 1))
            attn_grad = matmul(value_ref[row, col], stack(cot_ref[row, col]), (1, 1))
            raw.append((scores, attn_grad))
        low = []
        for scores, attn_grad in raw:
            exponent = jnp.exp(scores - jnp.max(scores, axis=0, keepdims=True))
            probs = exponent * (1.0 / jnp.sum(exponent, axis=0, keepdims=True))
            score_grad = probs * (attn_grad - jnp.sum(probs * attn_grad, axis=0, keepdims=True))
            low.append((probs.astype(BF16), score_grad.astype(BF16)))
        for (row, col), (probs, score_grad) in zip(group, low):
            value_grad = matmul(probs, stack(cot_ref[row, col]), (1, 0))
            key_grad = matmul(score_grad, stack(query_ref[row, col]), (1, 0))
            spread = matmul(score_grad, key_ref[row, col], (0, 0)) * mask
            query_grad = spread[:win_tokens]
            for head in range(1, BLOCK_HEADS):
                query_grad += spread[head * win_tokens : (head + 1) * win_tokens]
            for part, grad in enumerate((query_grad * scale, key_grad, value_grad)):
                base = part * width + col.start
                proj_ref[row, base : base + LANES] = grad.astype(BF16)


def first_kernel(halves, pos_ref, pixels_ref, weight_ref, proj_ref, normed_ref, term_ref, cot_ref, *scratch):
    channels = normed_ref.shape[1]
    side = 1 - lax.axis_index("rep") if halves > 1 else 0
    columns = half_slices(halves, side, channels)
    onehot = window_order(pos_ref)
    normed = matmul(onehot, pixels_ref[:, :channels], (1, 0)).astype(BF16)
    normed_ref[...] = normed
    start = pl.multiple_of(columns[0].start + channels, LANES)
    cot = pixels_ref[:, pl.ds(start, columns[0].size)]
    cot_ref[...] = matmul(onehot, cot, (1, 0)).astype(BF16)
    attend(weight_ref, columns, normed, (cot_ref, *scratch), proj_ref)
    term_ref[...] = matmul(normed, proj_ref[...], (0, 0)).astype(term_ref.dtype)


def second_kernel(pos_ref, pixels_ref, weight_ref, normed_ref, proj_ref, term_ref, cot_ref, *scratch):
    channels = normed_ref.shape[1]
    columns = half_slices(2, lax.axis_index("rep"), channels)
    start = pl.multiple_of(columns[0].start + channels, LANES)
    cot = pixels_ref[:, pl.ds(start, columns[0].size)]
    cot_ref[...] = matmul(window_order(pos_ref), cot, (1, 0)).astype(BF16)
    normed = normed_ref[...]
    attend(weight_ref, columns, normed, (cot_ref, *scratch), proj_ref)
    term_ref[...] = matmul(normed, proj_ref[...], (0, 0)).astype(BF16)


def back_kernel(pos_ref, weight_ref, *refs):
    *proj_refs, grad_ref = refs
    halves = len(proj_refs)
    channels = weight_ref.shape[0]
    width = channels // halves
    total = 0.0
    for index, ref in enumerate(proj_refs):
        side = lax.axis_index("rep") if halves > 1 else 0
        side = 1 - side if index == 0 and halves > 1 else side
        for part, column in enumerate(half_slices(halves, side, channels)):
            total += matmul(ref[:, part * width : (part + 1) * width], weight_ref[:, column], (1, 1))
    grad_ref[...] = matmul(window_order(pos_ref), total.astype(BF16), (0, 0)).astype(BF16)


def join_kernel(own_ref, other_ref, out_ref):
    width = own_ref.shape[1] // 3
    side = lax.axis_index("rep")
    for ref, half in ((own_ref, side), (other_ref, 1 - side)):
        for part in range(3):
            start = pl.multiple_of((2 * part + half) * width, LANES)
            out_ref[:, pl.ds(start, width)] = ref[:, part * width : (part + 1) * width]


def swap_reps(values):
    return lax.ppermute(values, "rep", [(0, 1), (1, 0)])


def split_kernel(axis, along, count, steps, *refs):
    me = lax.axis_index(axis)
    sources, parts = refs[:count], refs[count:]
    for step, ref in zip(steps, parts):
        index = (slice(None),) * along + (me ^ step,)
        ref[...] = sum(source[index].astype(F32) for source in sources).astype(BF16)


def split(axis, along, steps, name, *sources):
    shape = sources[0].shape
    part = jax.ShapeDtypeStruct(shape[:along] + shape[along + 1 :], BF16)
    kernel = functools.partial(split_kernel, axis, along, len(sources), steps)
    return vmem_call(kernel, [part] * len(steps), name, *sources)


def travel(parts, axis, steps):
    size = len(parts)
    return [parts[0]] + [
        lax.ppermute(part, axis, [(i, i ^ step) for i in range(size)])
        for part, step in zip(parts[1:], steps[1:])
    ]


def shards(tokens, qkv_weight, cotangent):
    rep_count = lax.axis_size("rep")
    row_tiles = lax.axis_size("ty")
    col_tiles = lax.axis_size("tx")
    tile_count = row_tiles * col_tiles
    _, tile_height, tile_width, channels = tokens.shape
    stride_rows = row_tiles * tile_height // GRID
    stride_cols = col_tiles * tile_width // GRID
    block_rows = min(tile_height, stride_rows)
    fold_rows = stride_rows // block_rows
    col_groups = tile_width // stride_cols
    outer_rows = tile_height // block_rows
    axes = ("tx", "rep", "ty") if rep_count == 2 else ("tx", "ty")
    samples = rep_count if "rep" in axes else 1
    group_count = tile_count * samples
    inner_rows = block_rows // group_count
    chunk = outer_rows * inner_rows * tile_width
    count = group_count * chunk

    cuts = {"tx": [("tx", col_tiles)], "rep": [("rep", samples)]}
    cuts["ty"] = [("ty", row_tiles // fold_rows), ("fold", fold_rows)]
    dims = [cut for axis in axes for cut in cuts[axis]]
    dims += [("outer", outer_rows), ("inner", inner_rows), ("group", col_groups), ("col", stride_cols)]
    names = [name for name, _ in dims]
    window = [name for name in ("rep", "fold", "inner", "col") if name in names]
    token = [name for name in names if name not in window]
    order = np.arange(count).reshape([size for _, size in dims])
    order = order.transpose([names.index(name) for name in window + token]).reshape(count)
    pos = np.zeros((1, count), np.int32)
    pos[0, order] = np.arange(count)

    local = (tile_height, tile_width, channels)
    split_shape = (outer_rows, group_count, inner_rows * tile_width)
    tokens, cotangent = tokens.reshape(local), cotangent.reshape(local)
    (sent,) = vmem_call(
        functools.partial(pack_kernel, split_shape),
        [jax.ShapeDtypeStruct((group_count, chunk, 2 * channels), BF16)],
        "pack",
        pltpu.with_memory_space_constraint(tokens, pltpu.HBM),
        pltpu.with_memory_space_constraint(cotangent, pltpu.HBM),
        scratch=[
            pltpu.VMEM(local, BF16),
            pltpu.VMEM(local, BF16),
            pltpu.SemaphoreType.DMA((2,)),
        ],
        remote=(0, 1),
    )
    pixels = lax.all_to_all(sent, axes, split_axis=0, concat_axis=0, tiled=True)
    pixels = pixels.reshape(count, 2 * channels)

    halves = 2 if rep_count == 2 else 1
    width = channels // halves
    order = jnp.asarray(pos)
    flat = jax.ShapeDtypeStruct((count, channels), BF16)
    proj = jax.ShapeDtypeStruct((count, 3 * width), BF16)
    term = jax.ShapeDtypeStruct((channels, 3 * width), BF16 if halves == 2 else F32)
    scratch = [pltpu.VMEM((count, width), BF16)] * 4
    first_proj, normed, send = vmem_call(
        functools.partial(first_kernel, halves),
        [proj, flat, term],
        "first_heads",
        order,
        pixels,
        qkv_weight,
        scratch=scratch,
        mib=16,
    )
    projs = [first_proj]
    if halves == 2:
        second_proj, keep = vmem_call(
            second_kernel,
            [proj, term],
            "second_heads",
            order,
            pixels,
            qkv_weight,
            normed,
            scratch=scratch,
            mib=16,
        )
        projs.append(second_proj)
        near = tuple(range(col_tiles))
        far = (0, 2, 3, 1)
        shape = (row_tiles, col_tiles, channels // tile_count, 3 * width)
        parts = split("tx", 1, near, "split_tx", keep.reshape(shape), swap_reps(send).reshape(shape))
    (normed_grad,) = vmem_call(back_kernel, [flat], "normed_grad", order, qkv_weight, *projs)
    spread = normed_grad.reshape(group_count, chunk, channels)
    returned = lax.all_to_all(spread, axes, split_axis=0, concat_axis=0, tiled=True)

    total = rep_count * tile_count
    if halves == 2:
        parts = split("ty", 0, far, "split_ty", *travel(parts, "tx", near))
        rows = sum(part.astype(F32) for part in travel(parts, "ty", far)) / total
        (weight_grad,) = vmem_call(
            join_kernel,
            [jax.ShapeDtypeStruct((rows.shape[0], 3 * channels), F32)],
            "weight_grad",
            rows,
            swap_reps(rows),
        )
    else:
        weight_grad = lax.psum_scatter(send, ("ty", "tx"), scatter_dimension=0, tiled=True)
        weight_grad = lax.psum(weight_grad, "rep") / total

    (token_grad,) = vmem_call(
        functools.partial(unpack_kernel, split_shape),
        [jax.ShapeDtypeStruct(local, BF16)],
        "token_grad",
        returned,
        tokens,
        cotangent,
    )
    token_grad = token_grad.reshape(1, *local)
    return (token_grad, weight_grad)


def solution(mesh):
    placed = (P("rep", "ty", "tx", None), P(), P("rep", "ty", "tx", None))
    return jax.shard_map(
        shards,
        mesh=mesh,
        in_specs=placed,
        out_specs=(P("rep", "ty", "tx", None), P(("ty", "tx"), None)),
        check_vma=False,
    )
```

```python
import functools

import jax
import jax.numpy as jnp
import numpy as np
from jax import lax
from jax.experimental import pallas as pl
from jax.experimental.pallas import tpu as pltpu
from jax.sharding import PartitionSpec as P

HEADS = 16
HEAD_DIM = 32
GRID = 8
EPS = 1e-05
LANES = 128
BLOCK_HEADS = LANES // HEAD_DIM
GROUP = 8

BF16 = jnp.bfloat16
F32 = jnp.float32


def matmul(a, b, contract):
    return lax.dot_general(a, b, ((contract[:1], contract[1:]), ((), ())), preferred_element_type=F32)


def normalize(pixels):
    center = pixels - jnp.mean(pixels, axis=-1, keepdims=True)
    inv_std = lax.rsqrt(jnp.mean(center * center, axis=-1, keepdims=True) + EPS)
    return center * inv_std, inv_std


def vmem_call(kernel, outs, name, *args, scratch=(), mib=8, remote=()):
    vmem = pl.BlockSpec(memory_space=pltpu.VMEM)
    hbm = pl.BlockSpec(memory_space=pltpu.HBM)
    return pl.pallas_call(
        kernel,
        out_shape=outs,
        in_specs=[hbm if index in remote else vmem for index in range(len(args))],
        out_specs=[vmem] * len(outs),
        scratch_shapes=scratch,
        compiler_params=pltpu.CompilerParams(vmem_limit_bytes=mib * 2**20),
        name=name,
    )(*args)


def in_chunks(shape, pixels):
    channels = pixels.shape[-1]
    pixels = pixels.astype(F32).reshape(*shape, channels)
    return jnp.concatenate([pixels[index] for index in range(shape[0])], axis=1)


def pack_kernel(shape, tokens_ref, cot_ref, sent_ref, tokens_buf, cot_buf, sems):
    channels = tokens_buf.shape[2]
    copies = [
        pltpu.make_async_copy(tokens_ref, tokens_buf, sems.at[0]),
        pltpu.make_async_copy(cot_ref, cot_buf, sems.at[1]),
    ]
    for copy in copies:
        copy.start()
    copies[0].wait()
    sent_ref[:, :, :channels] = normalize(in_chunks(shape, tokens_buf[...]))[0].astype(BF16)
    copies[1].wait()
    sent_ref[:, :, channels:] = in_chunks(shape, cot_buf[...]).astype(BF16)


def unpack_kernel(shape, returned_ref, tokens_ref, cot_ref, grad_ref):
    outer, tiles, size = shape
    standard, inv_std = normalize(in_chunks(shape, tokens_ref[...]))
    normed_grad = returned_ref[...].astype(F32)
    inner = (
        normed_grad
        - jnp.mean(normed_grad, axis=-1, keepdims=True)
        - standard * jnp.mean(normed_grad * standard, axis=-1, keepdims=True)
    )
    grad = in_chunks(shape, cot_ref[...]) + inv_std * inner
    rows = grad_ref.shape[0] // outer
    for index in range(outer):
        part = grad[:, index * size : (index + 1) * size].astype(BF16)
        grad_ref[index * rows : (index + 1) * rows] = part.reshape(rows, *grad_ref.shape[1:])


def window_order(pos_ref):
    count = pos_ref.shape[1]
    rows = lax.broadcasted_iota(jnp.int32, (count, count), 0)
    return jnp.where(rows == pos_ref[...], 1.0, 0.0).astype(BF16)


def half_slices(halves, side, channels):
    width = channels // halves
    return [pl.ds(pl.multiple_of(part * channels + side * width, LANES), width) for part in range(3)]


def attend(weight_ref, columns, normed, scratch, proj_ref):
    cot_ref, query_ref, key_ref, value_ref = scratch
    count, width = cot_ref.shape
    win_tokens = GRID * GRID
    scale = HEAD_DIM**-0.5

    query_ref[...] = (matmul(normed, weight_ref[:, columns[0]], (1, 0)) * scale).astype(BF16)
    key_ref[...] = matmul(normed, weight_ref[:, columns[1]], (1, 0)).astype(BF16)
    value_ref[...] = matmul(normed, weight_ref[:, columns[2]], (1, 0)).astype(BF16)

    stack_shape = (BLOCK_HEADS * win_tokens, LANES)
    own = lax.broadcasted_iota(jnp.int32, stack_shape, 0) // win_tokens == (
        lax.broadcasted_iota(jnp.int32, stack_shape, 1) // HEAD_DIM
    )
    mask = jnp.where(own, 1.0, 0.0)
    mask_low = mask.astype(BF16)

    def stack(block):
        return jnp.concatenate([block] * BLOCK_HEADS, axis=0) * mask_low

    cells = [
        (slice(row, row + win_tokens), slice(col, col + LANES))
        for row in range(0, count, win_tokens)
        for col in range(0, width, LANES)
    ]
    for first in range(0, len(cells), GROUP):
        group = cells[first : first + GROUP]
        raw = []
        for row, col in group:
            scores = matmul(key_ref[row, col], stack(query_ref[row, col]), (1, 1))
            attn_grad = matmul(value_ref[row, col], stack(cot_ref[row, col]), (1, 1))
            raw.append((scores, attn_grad))
        low = []
        for scores, attn_grad in raw:
            exponent = jnp.exp(scores - jnp.max(scores, axis=0, keepdims=True))
            probs = exponent * (1.0 / jnp.sum(exponent, axis=0, keepdims=True))
            score_grad = probs * (attn_grad - jnp.sum(probs * attn_grad, axis=0, keepdims=True))
            low.append((probs.astype(BF16), score_grad.astype(BF16)))
        for (row, col), (probs, score_grad) in zip(group, low):
            value_grad = matmul(probs, stack(cot_ref[row, col]), (1, 0))
            key_grad = matmul(score_grad, stack(query_ref[row, col]), (1, 0))
            spread = matmul(score_grad, key_ref[row, col], (0, 0)) * mask
            query_grad = spread[:win_tokens]
            for head in range(1, BLOCK_HEADS):
                query_grad += spread[head * win_tokens : (head + 1) * win_tokens]
            for part, grad in enumerate((query_grad * scale, key_grad, value_grad)):
                base = part * width + col.start
                proj_ref[row, base : base + LANES] = grad.astype(BF16)


def first_kernel(halves, pos_ref, pixels_ref, weight_ref, proj_ref, normed_ref, term_ref, cot_ref, *scratch):
    channels = normed_ref.shape[1]
    side = 1 - lax.axis_index("rep") if halves > 1 else 0
    columns = half_slices(halves, side, channels)
    onehot = window_order(pos_ref)
    normed = matmul(onehot, pixels_ref[:, :channels], (1, 0)).astype(BF16)
    normed_ref[...] = normed
    start = pl.multiple_of(columns[0].start + channels, LANES)
    cot = pixels_ref[:, pl.ds(start, columns[0].size)]
    cot_ref[...] = matmul(onehot, cot, (1, 0)).astype(BF16)
    attend(weight_ref, columns, normed, (cot_ref, *scratch), proj_ref)
    term_ref[...] = matmul(normed, proj_ref[...], (0, 0)).astype(term_ref.dtype)


def second_kernel(pos_ref, pixels_ref, weight_ref, normed_ref, proj_ref, term_ref, cot_ref, *scratch):
    channels = normed_ref.shape[1]
    columns = half_slices(2, lax.axis_index("rep"), channels)
    start = pl.multiple_of(columns[0].start + channels, LANES)
    cot = pixels_ref[:, pl.ds(start, columns[0].size)]
    cot_ref[...] = matmul(window_order(pos_ref), cot, (1, 0)).astype(BF16)
    normed = normed_ref[...]
    attend(weight_ref, columns, normed, (cot_ref, *scratch), proj_ref)
    term_ref[...] = matmul(normed, proj_ref[...], (0, 0)).astype(BF16)


def back_kernel(pos_ref, weight_ref, *refs):
    *proj_refs, grad_ref = refs
    halves = len(proj_refs)
    channels = weight_ref.shape[0]
    width = channels // halves
    total = 0.0
    for index, ref in enumerate(proj_refs):
        side = lax.axis_index("rep") if halves > 1 else 0
        side = 1 - side if index == 0 and halves > 1 else side
        for part, column in enumerate(half_slices(halves, side, channels)):
            total += matmul(ref[:, part * width : (part + 1) * width], weight_ref[:, column], (1, 1))
    grad_ref[...] = matmul(window_order(pos_ref), total.astype(BF16), (0, 0)).astype(BF16)


def join_kernel(own_ref, other_ref, out_ref):
    width = own_ref.shape[1] // 3
    side = lax.axis_index("rep")
    for ref, half in ((own_ref, side), (other_ref, 1 - side)):
        for part in range(3):
            start = pl.multiple_of((2 * part + half) * width, LANES)
            out_ref[:, pl.ds(start, width)] = ref[:, part * width : (part + 1) * width]


def swap_reps(values):
    return lax.ppermute(values, "rep", [(0, 1), (1, 0)])


def split_kernel(axis, along, count, steps, *refs):
    me = lax.axis_index(axis)
    sources, parts = refs[:count], refs[count:]
    for step, ref in zip(steps, parts):
        index = (slice(None),) * along + (me ^ step,)
        ref[...] = sum(source[index].astype(F32) for source in sources).astype(BF16)


def split(axis, along, steps, name, *sources):
    shape = sources[0].shape
    part = jax.ShapeDtypeStruct(shape[:along] + shape[along + 1 :], BF16)
    kernel = functools.partial(split_kernel, axis, along, len(sources), steps)
    return vmem_call(kernel, [part] * len(steps), name, *sources)


def travel(parts, axis, steps):
    size = len(parts)
    return [parts[0]] + [
        lax.ppermute(part, axis, [(i, i ^ step) for i in range(size)])
        for part, step in zip(parts[1:], steps[1:])
    ]


def shards(tokens, qkv_weight, cotangent):
    rep_count = lax.axis_size("rep")
    row_tiles = lax.axis_size("ty")
    col_tiles = lax.axis_size("tx")
    tile_count = row_tiles * col_tiles
    _, tile_height, tile_width, channels = tokens.shape
    stride_rows = row_tiles * tile_height // GRID
    stride_cols = col_tiles * tile_width // GRID
    block_rows = min(tile_height, stride_rows)
    fold_rows = stride_rows // block_rows
    col_groups = tile_width // stride_cols
    outer_rows = tile_height // block_rows
    samples = rep_count if rep_count == 2 and fold_rows == 1 else 1
    group_count = tile_count * samples
    digits = {"rep": samples, "z": row_tiles // 2, "row": 2, "y": col_tiles // 2, "column": 2}
    natural = list(digits)
    turned = ["y", "column", "row", "rep", "z"] if samples == 2 else natural
    devices = np.arange(group_count).reshape(list(digits.values()))
    devices = devices.transpose([natural.index(name) for name in turned]).reshape(-1).tolist()
    groups = [[rep * tile_count + device for device in devices] for rep in range(rep_count // samples)]
    exchange = functools.partial(
        lax.all_to_all,
        axis_name=("rep", "ty", "tx"),
        split_axis=0,
        concat_axis=0,
        tiled=True,
        axis_index_groups=groups,
    )
    inner_rows = block_rows // group_count
    chunk = outer_rows * inner_rows * tile_width
    count = group_count * chunk

    dims = [(name, digits[name]) for name in turned]
    dims += [("outer", outer_rows), ("inner", inner_rows), ("group", col_groups), ("col", stride_cols)]
    names = [name for name, _ in dims]
    window = ["rep", "inner", "col"] + ["row"] * (fold_rows == 2)
    token = [name for name in names if name not in window]
    order = np.arange(count).reshape([size for _, size in dims])
    order = order.transpose([names.index(name) for name in window + token]).reshape(count)
    pos = np.zeros((1, count), np.int32)
    pos[0, order] = np.arange(count)

    local = (tile_height, tile_width, channels)
    split_shape = (outer_rows, group_count, inner_rows * tile_width)
    tokens, cotangent = tokens.reshape(local), cotangent.reshape(local)
    (sent,) = vmem_call(
        functools.partial(pack_kernel, split_shape),
        [jax.ShapeDtypeStruct((group_count, chunk, 2 * channels), BF16)],
        "pack",
        pltpu.with_memory_space_constraint(tokens, pltpu.HBM),
        pltpu.with_memory_space_constraint(cotangent, pltpu.HBM),
        scratch=[
            pltpu.VMEM(local, BF16),
            pltpu.VMEM(local, BF16),
            pltpu.SemaphoreType.DMA((2,)),
        ],
        remote=(0, 1),
    )
    pixels = exchange(sent)
    pixels = pixels.reshape(count, 2 * channels)

    halves = samples
    width = channels // halves
    order = jnp.asarray(pos)
    flat = jax.ShapeDtypeStruct((count, channels), BF16)
    proj = jax.ShapeDtypeStruct((count, 3 * width), BF16)
    term = jax.ShapeDtypeStruct((channels, 3 * width), BF16 if halves == 2 else F32)
    scratch = [pltpu.VMEM((count, width), BF16)] * 4
    first_proj, normed, send = vmem_call(
        functools.partial(first_kernel, halves),
        [proj, flat, term],
        "first_heads",
        order,
        pixels,
        qkv_weight,
        scratch=scratch,
        mib=16,
    )
    projs = [first_proj]
    if halves == 2:
        second_proj, keep = vmem_call(
            second_kernel,
            [proj, term],
            "second_heads",
            order,
            pixels,
            qkv_weight,
            normed,
            scratch=scratch,
            mib=16,
        )
        projs.append(second_proj)
        near = tuple(range(col_tiles))
        far = (0, 2, 3, 1)
        shape = (row_tiles, col_tiles, channels // tile_count, 3 * width)
        parts = split("tx", 1, near, "split_tx", keep.reshape(shape), swap_reps(send).reshape(shape))
    (normed_grad,) = vmem_call(back_kernel, [flat], "normed_grad", order, qkv_weight, *projs)
    spread = normed_grad.reshape(group_count, chunk, channels)
    returned = exchange(spread)

    total = rep_count * tile_count
    if halves == 2:
        parts = split("ty", 0, far, "split_ty", *travel(parts, "tx", near))
        rows = sum(part.astype(F32) for part in travel(parts, "ty", far)) / total
        (weight_grad,) = vmem_call(
            join_kernel,
            [jax.ShapeDtypeStruct((rows.shape[0], 3 * channels), F32)],
            "weight_grad",
            rows,
            swap_reps(rows),
        )
    else:
        weight_grad = lax.psum_scatter(send, ("ty", "tx"), scatter_dimension=0, tiled=True)
        weight_grad = lax.psum(weight_grad, "rep") / total

    (token_grad,) = vmem_call(
        functools.partial(unpack_kernel, split_shape),
        [jax.ShapeDtypeStruct(local, BF16)],
        "token_grad",
        returned,
        tokens,
        cotangent,
    )
    token_grad = token_grad.reshape(1, *local)
    return (token_grad, weight_grad)


def solution(mesh):
    placed = (P("rep", "ty", "tx", None), P(), P("rep", "ty", "tx", None))
    return jax.shard_map(
        shards,
        mesh=mesh,
        in_specs=placed,
        out_specs=(P("rep", "ty", "tx", None), P(("ty", "tx"), None)),
        check_vma=False,
    )
```

```python
import functools

import jax
import jax.numpy as jnp
import numpy as np
from jax import lax
from jax.experimental import pallas as pl
from jax.experimental.pallas import tpu as pltpu
from jax.sharding import PartitionSpec as P

HEADS = 16
HEAD_DIM = 32
GRID = 8
EPS = 1e-05
LANES = 128
BLOCK_HEADS = LANES // HEAD_DIM
GROUP = 8

BF16 = jnp.bfloat16
F32 = jnp.float32


def matmul(a, b, contract):
    return lax.dot_general(a, b, ((contract[:1], contract[1:]), ((), ())), preferred_element_type=F32)


def normalize(pixels):
    center = pixels - jnp.mean(pixels, axis=-1, keepdims=True)
    inv_std = lax.rsqrt(jnp.mean(center * center, axis=-1, keepdims=True) + EPS)
    return center * inv_std, inv_std


def vmem_call(kernel, outs, name, *args, scratch=(), mib=8, remote=()):
    vmem = pl.BlockSpec(memory_space=pltpu.VMEM)
    hbm = pl.BlockSpec(memory_space=pltpu.HBM)
    return pl.pallas_call(
        kernel,
        out_shape=outs,
        in_specs=[hbm if index in remote else vmem for index in range(len(args))],
        out_specs=[vmem] * len(outs),
        scratch_shapes=scratch,
        compiler_params=pltpu.CompilerParams(vmem_limit_bytes=mib * 2**20),
        name=name,
    )(*args)


def in_chunks(shape, pixels):
    channels = pixels.shape[-1]
    pixels = pixels.astype(F32).reshape(*shape, channels)
    return jnp.concatenate([pixels[index] for index in range(shape[0])], axis=1)


def pack_kernel(shape, tokens_ref, cot_ref, sent_ref, tokens_buf, cot_buf, sems):
    channels = tokens_buf.shape[2]
    copies = [
        pltpu.make_async_copy(tokens_ref, tokens_buf, sems.at[0]),
        pltpu.make_async_copy(cot_ref, cot_buf, sems.at[1]),
    ]
    for copy in copies:
        copy.start()
    copies[0].wait()
    sent_ref[:, :, :channels] = normalize(in_chunks(shape, tokens_buf[...]))[0].astype(BF16)
    copies[1].wait()
    sent_ref[:, :, channels:] = in_chunks(shape, cot_buf[...]).astype(BF16)


def unpack_kernel(shape, returned_ref, tokens_ref, cot_ref, grad_ref):
    outer, tiles, size = shape
    standard, inv_std = normalize(in_chunks(shape, tokens_ref[...]))
    normed_grad = returned_ref[...].astype(F32)
    inner = (
        normed_grad
        - jnp.mean(normed_grad, axis=-1, keepdims=True)
        - standard * jnp.mean(normed_grad * standard, axis=-1, keepdims=True)
    )
    grad = in_chunks(shape, cot_ref[...]) + inv_std * inner
    rows = grad_ref.shape[0] // outer
    for index in range(outer):
        part = grad[:, index * size : (index + 1) * size].astype(BF16)
        grad_ref[index * rows : (index + 1) * rows] = part.reshape(rows, *grad_ref.shape[1:])


def window_order(pos_ref):
    count = pos_ref.shape[1]
    rows = lax.broadcasted_iota(jnp.int32, (count, count), 0)
    return jnp.where(rows == pos_ref[...], 1.0, 0.0).astype(BF16)


def half_slices(halves, side, channels):
    width = channels // halves
    return [pl.ds(pl.multiple_of(part * channels + side * width, LANES), width) for part in range(3)]


def attend(weight_ref, columns, normed, scratch, proj_ref):
    cot_ref, query_ref, key_ref, value_ref = scratch
    count, width = cot_ref.shape
    win_tokens = GRID * GRID
    scale = HEAD_DIM**-0.5

    query_ref[...] = (matmul(normed, weight_ref[:, columns[0]], (1, 0)) * scale).astype(BF16)
    key_ref[...] = matmul(normed, weight_ref[:, columns[1]], (1, 0)).astype(BF16)
    value_ref[...] = matmul(normed, weight_ref[:, columns[2]], (1, 0)).astype(BF16)

    stack_shape = (BLOCK_HEADS * win_tokens, LANES)
    own = lax.broadcasted_iota(jnp.int32, stack_shape, 0) // win_tokens == (
        lax.broadcasted_iota(jnp.int32, stack_shape, 1) // HEAD_DIM
    )
    mask = jnp.where(own, 1.0, 0.0)
    mask_low = mask.astype(BF16)

    def stack(block):
        return jnp.concatenate([block] * BLOCK_HEADS, axis=0) * mask_low

    cells = [
        (slice(row, row + win_tokens), slice(col, col + LANES))
        for row in range(0, count, win_tokens)
        for col in range(0, width, LANES)
    ]
    for first in range(0, len(cells), GROUP):
        group = cells[first : first + GROUP]
        raw = []
        for row, col in group:
            scores = matmul(key_ref[row, col], stack(query_ref[row, col]), (1, 1))
            attn_grad = matmul(value_ref[row, col], stack(cot_ref[row, col]), (1, 1))
            raw.append((scores, attn_grad))
        low = []
        for scores, attn_grad in raw:
            exponent = jnp.exp(scores - jnp.max(scores, axis=0, keepdims=True))
            probs = exponent * (1.0 / jnp.sum(exponent, axis=0, keepdims=True))
            score_grad = probs * (attn_grad - jnp.sum(probs * attn_grad, axis=0, keepdims=True))
            low.append((probs.astype(BF16), score_grad.astype(BF16)))
        for (row, col), (probs, score_grad) in zip(group, low):
            value_grad = matmul(probs, stack(cot_ref[row, col]), (1, 0))
            key_grad = matmul(score_grad, stack(query_ref[row, col]), (1, 0))
            spread = matmul(score_grad, key_ref[row, col], (0, 0)) * mask
            query_grad = spread[:win_tokens]
            for head in range(1, BLOCK_HEADS):
                query_grad += spread[head * win_tokens : (head + 1) * win_tokens]
            for part, grad in enumerate((query_grad * scale, key_grad, value_grad)):
                base = part * width + col.start
                proj_ref[row, base : base + LANES] = grad.astype(BF16)


def first_kernel(halves, pos_ref, pixels_ref, weight_ref, proj_ref, normed_ref, term_ref, cot_ref, *scratch):
    channels = normed_ref.shape[1]
    side = 1 - lax.axis_index("rep") if halves > 1 else 0
    columns = half_slices(halves, side, channels)
    onehot = window_order(pos_ref)
    normed = matmul(onehot, pixels_ref[:, :channels], (1, 0)).astype(BF16)
    normed_ref[...] = normed
    start = pl.multiple_of(columns[0].start + channels, LANES)
    cot = pixels_ref[:, pl.ds(start, columns[0].size)]
    cot_ref[...] = matmul(onehot, cot, (1, 0)).astype(BF16)
    attend(weight_ref, columns, normed, (cot_ref, *scratch), proj_ref)
    term_ref[...] = matmul(normed, proj_ref[...], (0, 0)).astype(term_ref.dtype)


def input_grad(weight_ref, columns, proj_ref):
    width = columns[0].size
    return sum(
        matmul(proj_ref[:, part * width : (part + 1) * width], weight_ref[:, column], (1, 1))
        for part, column in enumerate(columns)
    )


def second_kernel(
    pos_ref, pixels_ref, weight_ref, first_ref, normed_ref, grad_ref, term_ref, proj_ref, cot_ref, *scratch
):
    channels = normed_ref.shape[1]
    side = lax.axis_index("rep")
    columns = half_slices(2, side, channels)
    start = pl.multiple_of(columns[0].start + channels, LANES)
    cot = pixels_ref[:, pl.ds(start, columns[0].size)]
    cot_ref[...] = matmul(window_order(pos_ref), cot, (1, 0)).astype(BF16)
    normed = normed_ref[...]
    attend(weight_ref, columns, normed, (cot_ref, *scratch), proj_ref)
    grad = input_grad(weight_ref, columns, proj_ref)
    grad += input_grad(weight_ref, half_slices(2, 1 - side, channels), first_ref)
    grad_ref[...] = grad.astype(BF16)
    term_ref[...] = matmul(normed, proj_ref[...], (0, 0)).astype(BF16)


def back_kernel(weight_ref, proj_ref, grad_ref):
    grad_ref[...] = matmul(proj_ref[...], weight_ref[...], (1, 1)).astype(BF16)


def spread_kernel(pos_ref, grad_ref, out_ref):
    out_ref[...] = matmul(window_order(pos_ref), grad_ref[...], (0, 0)).astype(BF16)


def join_kernel(own_ref, other_ref, out_ref):
    width = own_ref.shape[1] // 3
    side = lax.axis_index("rep")
    for ref, half in ((own_ref, side), (other_ref, 1 - side)):
        for part in range(3):
            start = pl.multiple_of((2 * part + half) * width, LANES)
            out_ref[:, pl.ds(start, width)] = ref[:, part * width : (part + 1) * width]


def swap_reps(values):
    return lax.ppermute(values, "rep", [(0, 1), (1, 0)])


def split_kernel(axis, along, count, steps, *refs):
    me = lax.axis_index(axis)
    sources, parts = refs[:count], refs[count:]
    for step, ref in zip(steps, parts):
        index = (slice(None),) * along + (me ^ step,)
        ref[...] = sum(source[index].astype(F32) for source in sources).astype(BF16)


def split(axis, along, steps, name, *sources):
    shape = sources[0].shape
    part = jax.ShapeDtypeStruct(shape[:along] + shape[along + 1 :], BF16)
    kernel = functools.partial(split_kernel, axis, along, len(sources), steps)
    return vmem_call(kernel, [part] * len(steps), name, *sources)


def travel(parts, axis, steps):
    size = len(parts)
    return [parts[0]] + [
        lax.ppermute(part, axis, [(i, i ^ step) for i in range(size)])
        for part, step in zip(parts[1:], steps[1:])
    ]


def shards(tokens, qkv_weight, cotangent):
    rep_count = lax.axis_size("rep")
    row_tiles = lax.axis_size("ty")
    col_tiles = lax.axis_size("tx")
    tile_count = row_tiles * col_tiles
    _, tile_height, tile_width, channels = tokens.shape
    stride_rows = row_tiles * tile_height // GRID
    stride_cols = col_tiles * tile_width // GRID
    block_rows = min(tile_height, stride_rows)
    fold_rows = stride_rows // block_rows
    col_groups = tile_width // stride_cols
    outer_rows = tile_height // block_rows
    samples = rep_count if rep_count == 2 and fold_rows == 1 else 1
    group_count = tile_count * samples
    digits = {"rep": samples, "z": row_tiles // 2, "row": 2, "y": col_tiles // 2, "column": 2}
    natural = list(digits)
    turned = ["y", "column", "row", "rep", "z"] if samples == 2 else natural
    devices = np.arange(group_count).reshape(list(digits.values()))
    devices = devices.transpose([natural.index(name) for name in turned]).reshape(-1).tolist()
    groups = [[rep * tile_count + device for device in devices] for rep in range(rep_count // samples)]
    exchange = functools.partial(
        lax.all_to_all,
        axis_name=("rep", "ty", "tx"),
        split_axis=0,
        concat_axis=0,
        tiled=True,
        axis_index_groups=groups,
    )
    inner_rows = block_rows // group_count
    chunk = outer_rows * inner_rows * tile_width
    count = group_count * chunk

    dims = [(name, digits[name]) for name in turned]
    dims += [("outer", outer_rows), ("inner", inner_rows), ("group", col_groups), ("col", stride_cols)]
    names = [name for name, _ in dims]
    window = ["rep", "inner", "col"] + ["row"] * (fold_rows == 2)
    token = [name for name in names if name not in window]
    order = np.arange(count).reshape([size for _, size in dims])
    order = order.transpose([names.index(name) for name in window + token]).reshape(count)
    pos = np.zeros((1, count), np.int32)
    pos[0, order] = np.arange(count)

    local = (tile_height, tile_width, channels)
    split_shape = (outer_rows, group_count, inner_rows * tile_width)
    tokens, cotangent = tokens.reshape(local), cotangent.reshape(local)
    (sent,) = vmem_call(
        functools.partial(pack_kernel, split_shape),
        [jax.ShapeDtypeStruct((group_count, chunk, 2 * channels), BF16)],
        "pack",
        pltpu.with_memory_space_constraint(tokens, pltpu.HBM),
        pltpu.with_memory_space_constraint(cotangent, pltpu.HBM),
        scratch=[
            pltpu.VMEM(local, BF16),
            pltpu.VMEM(local, BF16),
            pltpu.SemaphoreType.DMA((2,)),
        ],
        remote=(0, 1),
    )
    pixels = exchange(sent)
    pixels = pixels.reshape(count, 2 * channels)

    halves = samples
    width = channels // halves
    order = jnp.asarray(pos)
    flat = jax.ShapeDtypeStruct((count, channels), BF16)
    proj = jax.ShapeDtypeStruct((count, 3 * width), BF16)
    term = jax.ShapeDtypeStruct((channels, 3 * width), BF16 if halves == 2 else F32)
    scratch = [pltpu.VMEM((count, width), BF16)] * 4
    first_proj, normed, send = vmem_call(
        functools.partial(first_kernel, halves),
        [proj, flat, term],
        "first_heads",
        order,
        pixels,
        qkv_weight,
        scratch=scratch,
        mib=16,
    )
    if halves == 2:
        grad, keep = vmem_call(
            second_kernel,
            [flat, term],
            "second_heads",
            order,
            pixels,
            qkv_weight,
            first_proj,
            normed,
            scratch=[pltpu.VMEM((count, 3 * width), BF16)] + scratch,
            mib=16,
        )
        near = tuple(range(col_tiles))
        far = (0, 1, 2, 3)
        shape = (row_tiles, col_tiles, channels // tile_count, 3 * width)
        parts = split("tx", 1, near, "split_tx", keep.reshape(shape), swap_reps(send).reshape(shape))
    else:
        (grad,) = vmem_call(back_kernel, [flat], "normed_grad", qkv_weight, first_proj)
    (normed_grad,) = vmem_call(spread_kernel, [flat], "spread", order, grad)
    spread = normed_grad.reshape(group_count, chunk, channels)
    returned = exchange(spread)

    total = rep_count * tile_count
    if halves == 2:
        parts = split("ty", 0, far, "split_ty", *travel(parts, "tx", near))
        rows = sum(part.astype(F32) for part in travel(parts, "ty", far)) / total
        (weight_grad,) = vmem_call(
            join_kernel,
            [jax.ShapeDtypeStruct((rows.shape[0], 3 * channels), F32)],
            "weight_grad",
            rows,
            swap_reps(rows),
        )
    else:
        weight_grad = lax.psum_scatter(send, ("ty", "tx"), scatter_dimension=0, tiled=True)
        weight_grad = lax.psum(weight_grad, "rep") / total

    (token_grad,) = vmem_call(
        functools.partial(unpack_kernel, split_shape),
        [jax.ShapeDtypeStruct(local, BF16)],
        "token_grad",
        returned,
        tokens,
        cotangent,
    )
    token_grad = token_grad.reshape(1, *local)
    return (token_grad, weight_grad)


def solution(mesh):
    placed = (P("rep", "ty", "tx", None), P(), P("rep", "ty", "tx", None))
    return jax.shard_map(
        shards,
        mesh=mesh,
        in_specs=placed,
        out_specs=(P("rep", "ty", "tx", None), P(("ty", "tx"), None)),
        check_vma=False,
    )
```

```python
import functools

import jax
import jax.numpy as jnp
import numpy as np
from jax import lax
from jax.experimental import pallas as pl
from jax.experimental.pallas import tpu as pltpu
from jax.sharding import PartitionSpec as P

HEAD_DIM = 32
GRID = 8
EPS = 1e-05
LANES = 128
BLOCK_HEADS = LANES // HEAD_DIM
GROUP = 8

BF16 = jnp.bfloat16
F32 = jnp.float32


def matmul(a, b, contract):
    return lax.dot_general(a, b, ((contract[:1], contract[1:]), ((), ())), preferred_element_type=F32)


def normalize(pixels):
    center = pixels - jnp.mean(pixels, axis=-1, keepdims=True)
    inv_std = lax.rsqrt(jnp.mean(center * center, axis=-1, keepdims=True) + EPS)
    return center * inv_std, inv_std


def vmem_call(kernel, outs, name, *args, scratch=(), mib=8, remote=()):
    vmem = pl.BlockSpec(memory_space=pltpu.VMEM)
    hbm = pl.BlockSpec(memory_space=pltpu.HBM)
    return pl.pallas_call(
        kernel,
        out_shape=outs,
        in_specs=[hbm if index in remote else vmem for index in range(len(args))],
        out_specs=[vmem] * len(outs),
        scratch_shapes=scratch,
        compiler_params=pltpu.CompilerParams(vmem_limit_bytes=mib * 2**20),
        name=name,
    )(*args)


def in_chunks(shape, pixels):
    channels = pixels.shape[-1]
    pixels = pixels.astype(F32).reshape(*shape, channels)
    return jnp.concatenate([pixels[index] for index in range(shape[0])], axis=1)


def pack_kernel(shape, tokens_ref, cot_ref, sent_ref, tokens_buf, cot_buf, sems):
    channels = tokens_buf.shape[2]
    copies = [
        pltpu.make_async_copy(tokens_ref, tokens_buf, sems.at[0]),
        pltpu.make_async_copy(cot_ref, cot_buf, sems.at[1]),
    ]
    for copy in copies:
        copy.start()
    copies[0].wait()
    sent_ref[:, :, :channels] = normalize(in_chunks(shape, tokens_buf[...]))[0].astype(BF16)
    copies[1].wait()
    sent_ref[:, :, channels:] = in_chunks(shape, cot_buf[...]).astype(BF16)


def unpack_kernel(shape, returned_ref, tokens_ref, cot_ref, grad_ref):
    outer, tiles, size = shape
    standard, inv_std = normalize(in_chunks(shape, tokens_ref[...]))
    normed_grad = returned_ref[...].astype(F32)
    inner = (
        normed_grad
        - jnp.mean(normed_grad, axis=-1, keepdims=True)
        - standard * jnp.mean(normed_grad * standard, axis=-1, keepdims=True)
    )
    grad = in_chunks(shape, cot_ref[...]) + inv_std * inner
    rows = grad_ref.shape[0] // outer
    for index in range(outer):
        part = grad[:, index * size : (index + 1) * size].astype(BF16)
        grad_ref[index * rows : (index + 1) * rows] = part.reshape(rows, *grad_ref.shape[1:])


def window_order(pos_ref):
    count = pos_ref.shape[1]
    rows = lax.broadcasted_iota(jnp.int32, (count, count), 0)
    return jnp.where(rows == pos_ref[...], 1.0, 0.0).astype(BF16)


def half_slices(halves, side, channels):
    width = channels // halves
    return [pl.ds(pl.multiple_of(part * channels + side * width, LANES), width) for part in range(3)]


def attend(weight_ref, columns, normed, scratch, proj_ref):
    cot_ref, query_ref, key_ref, value_ref = scratch
    count, width = cot_ref.shape
    win_tokens = GRID * GRID
    scale = HEAD_DIM**-0.5

    query_ref[...] = (matmul(normed, weight_ref[:, columns[0]], (1, 0)) * scale).astype(BF16)
    key_ref[...] = matmul(normed, weight_ref[:, columns[1]], (1, 0)).astype(BF16)
    value_ref[...] = matmul(normed, weight_ref[:, columns[2]], (1, 0)).astype(BF16)

    stack_shape = (BLOCK_HEADS * win_tokens, LANES)
    own = lax.broadcasted_iota(jnp.int32, stack_shape, 0) // win_tokens == (
        lax.broadcasted_iota(jnp.int32, stack_shape, 1) // HEAD_DIM
    )
    mask = jnp.where(own, 1.0, 0.0)
    mask_low = mask.astype(BF16)

    def stack(block):
        return jnp.concatenate([block] * BLOCK_HEADS, axis=0) * mask_low

    cells = [
        (slice(row, row + win_tokens), slice(col, col + LANES))
        for row in range(0, count, win_tokens)
        for col in range(0, width, LANES)
    ]
    for first in range(0, len(cells), GROUP):
        group = cells[first : first + GROUP]
        stacks = [(stack(query_ref[row, col]), stack(cot_ref[row, col])) for row, col in group]
        raw = []
        for (row, col), (queries, cots) in zip(group, stacks):
            scores = matmul(key_ref[row, col], queries, (1, 1))
            attn_grad = matmul(value_ref[row, col], cots, (1, 1))
            raw.append((scores, attn_grad))
        low = []
        for scores, attn_grad in raw:
            exponent = jnp.exp(scores - jnp.max(scores, axis=0, keepdims=True))
            probs = exponent * (1.0 / jnp.sum(exponent, axis=0, keepdims=True))
            score_grad = probs * (attn_grad - jnp.sum(probs * attn_grad, axis=0, keepdims=True))
            low.append((probs.astype(BF16), score_grad.astype(BF16)))
        for (row, col), (probs, score_grad), (queries, cots) in zip(group, low, stacks):
            value_grad = matmul(probs, cots, (1, 0))
            key_grad = matmul(score_grad, queries, (1, 0))
            spread = matmul(score_grad, key_ref[row, col], (0, 0)) * mask
            query_grad = spread[:win_tokens]
            for head in range(1, BLOCK_HEADS):
                query_grad += spread[head * win_tokens : (head + 1) * win_tokens]
            for part, grad in enumerate((query_grad * scale, key_grad, value_grad)):
                base = part * width + col.start
                proj_ref[row, base : base + LANES] = grad.astype(BF16)


def first_kernel(halves, pos_ref, pixels_ref, weight_ref, proj_ref, normed_ref, term_ref, cot_ref, *scratch):
    channels = normed_ref.shape[1]
    side = 1 - lax.axis_index("rep") if halves > 1 else 0
    columns = half_slices(halves, side, channels)
    onehot = window_order(pos_ref)
    normed = matmul(onehot, pixels_ref[:, :channels], (1, 0)).astype(BF16)
    normed_ref[...] = normed
    start = pl.multiple_of(columns[0].start + channels, LANES)
    cot = pixels_ref[:, pl.ds(start, columns[0].size)]
    cot_ref[...] = matmul(onehot, cot, (1, 0)).astype(BF16)
    attend(weight_ref, columns, normed, (cot_ref, *scratch), proj_ref)
    term_ref[...] = matmul(normed, proj_ref[...], (0, 0)).astype(term_ref.dtype)


def input_grad(weight_ref, columns, proj_ref):
    width = columns[0].size
    return sum(
        matmul(proj_ref[:, part * width : (part + 1) * width], weight_ref[:, column], (1, 1))
        for part, column in enumerate(columns)
    )


def second_kernel(
    pos_ref, pixels_ref, weight_ref, first_ref, normed_ref, grad_ref, term_ref, proj_ref, cot_ref, *scratch
):
    channels = normed_ref.shape[1]
    side = lax.axis_index("rep")
    columns = half_slices(2, side, channels)
    start = pl.multiple_of(columns[0].start + channels, LANES)
    cot = pixels_ref[:, pl.ds(start, columns[0].size)]
    cot_ref[...] = matmul(window_order(pos_ref), cot, (1, 0)).astype(BF16)
    normed = normed_ref[...]
    attend(weight_ref, columns, normed, (cot_ref, *scratch), proj_ref)
    grad = input_grad(weight_ref, columns, proj_ref)
    grad += input_grad(weight_ref, half_slices(2, 1 - side, channels), first_ref)
    grad_ref[...] = grad.astype(BF16)
    term_ref[...] = matmul(normed, proj_ref[...], (0, 0)).astype(BF16)


def back_kernel(weight_ref, proj_ref, grad_ref):
    grad_ref[...] = matmul(proj_ref[...], weight_ref[...], (1, 1)).astype(BF16)


def spread_kernel(pos_ref, grad_ref, out_ref):
    out_ref[...] = matmul(window_order(pos_ref), grad_ref[...], (0, 0)).astype(BF16)


def join_kernel(own_ref, other_ref, out_ref):
    width = own_ref.shape[1] // 3
    side = lax.axis_index("rep")
    for ref, half in ((own_ref, side), (other_ref, 1 - side)):
        for part in range(3):
            start = pl.multiple_of((2 * part + half) * width, LANES)
            out_ref[:, pl.ds(start, width)] = ref[:, part * width : (part + 1) * width]


def swap_reps(values):
    return lax.ppermute(values, "rep", [(0, 1), (1, 0)])


def split_kernel(axis, along, count, steps, *refs):
    me = lax.axis_index(axis)
    sources, parts = refs[:count], refs[count:]
    for step, ref in zip(steps, parts):
        index = (slice(None),) * along + (me ^ step,)
        ref[...] = sum(source[index].astype(F32) for source in sources).astype(BF16)


def split(axis, along, steps, name, *sources):
    shape = sources[0].shape
    part = jax.ShapeDtypeStruct(shape[:along] + shape[along + 1 :], BF16)
    kernel = functools.partial(split_kernel, axis, along, len(sources), steps)
    return vmem_call(kernel, [part] * len(steps), name, *sources)


def travel(parts, axis, steps):
    size = len(parts)
    return [parts[0]] + [
        lax.ppermute(part, axis, [(i, i ^ step) for i in range(size)])
        for part, step in zip(parts[1:], steps[1:])
    ]


def shards(tokens, qkv_weight, cotangent):
    rep_count = lax.axis_size("rep")
    row_tiles = lax.axis_size("ty")
    col_tiles = lax.axis_size("tx")
    tile_count = row_tiles * col_tiles
    _, tile_height, tile_width, channels = tokens.shape
    stride_rows = row_tiles * tile_height // GRID
    stride_cols = col_tiles * tile_width // GRID
    block_rows = min(tile_height, stride_rows)
    fold_rows = stride_rows // block_rows
    col_groups = tile_width // stride_cols
    outer_rows = tile_height // block_rows
    samples = rep_count if rep_count == 2 and fold_rows == 1 else 1
    group_count = tile_count * samples
    digits = {"rep": samples, "z": row_tiles // 2, "row": 2, "y": col_tiles // 2, "column": 2}
    natural = list(digits)
    turned = ["y", "column", "row", "rep", "z"] if samples == 2 else natural
    devices = np.arange(group_count).reshape(list(digits.values()))
    devices = devices.transpose([natural.index(name) for name in turned]).reshape(-1).tolist()
    groups = [[rep * tile_count + device for device in devices] for rep in range(rep_count // samples)]
    exchange = functools.partial(
        lax.all_to_all,
        axis_name=("rep", "ty", "tx"),
        split_axis=0,
        concat_axis=0,
        tiled=True,
        axis_index_groups=groups,
    )
    inner_rows = block_rows // group_count
    chunk = outer_rows * inner_rows * tile_width
    count = group_count * chunk

    dims = [(name, digits[name]) for name in turned]
    dims += [("outer", outer_rows), ("inner", inner_rows), ("group", col_groups), ("col", stride_cols)]
    names = [name for name, _ in dims]
    window = ["rep", "inner", "col"] + ["row"] * (fold_rows == 2)
    token = [name for name in names if name not in window]
    order = np.arange(count).reshape([size for _, size in dims])
    order = order.transpose([names.index(name) for name in window + token]).reshape(count)
    pos = np.zeros((1, count), np.int32)
    pos[0, order] = np.arange(count)

    local = (tile_height, tile_width, channels)
    split_shape = (outer_rows, group_count, inner_rows * tile_width)
    tokens, cotangent = tokens.reshape(local), cotangent.reshape(local)
    (sent,) = vmem_call(
        functools.partial(pack_kernel, split_shape),
        [jax.ShapeDtypeStruct((group_count, chunk, 2 * channels), BF16)],
        "pack",
        pltpu.with_memory_space_constraint(tokens, pltpu.HBM),
        pltpu.with_memory_space_constraint(cotangent, pltpu.HBM),
        scratch=[
            pltpu.VMEM(local, BF16),
            pltpu.VMEM(local, BF16),
            pltpu.SemaphoreType.DMA((2,)),
        ],
        remote=(0, 1),
    )
    pixels = exchange(sent)
    pixels = pixels.reshape(count, 2 * channels)

    halves = samples
    width = channels // halves
    order = jnp.asarray(pos)
    flat = jax.ShapeDtypeStruct((count, channels), BF16)
    proj = jax.ShapeDtypeStruct((count, 3 * width), BF16)
    term = jax.ShapeDtypeStruct((channels, 3 * width), BF16 if halves == 2 else F32)
    scratch = [pltpu.VMEM((count, width), BF16)] * 4
    first_proj, normed, send = vmem_call(
        functools.partial(first_kernel, halves),
        [proj, flat, term],
        "first_heads",
        order,
        pixels,
        qkv_weight,
        scratch=scratch,
        mib=16,
    )
    if halves == 2:
        grad, keep = vmem_call(
            second_kernel,
            [flat, term],
            "second_heads",
            order,
            pixels,
            qkv_weight,
            first_proj,
            normed,
            scratch=[pltpu.VMEM((count, 3 * width), BF16)] + scratch,
            mib=16,
        )
        near = tuple(range(col_tiles))
        far = tuple(range(row_tiles))
        shape = (row_tiles, col_tiles, channels // tile_count, 3 * width)
        parts = split("tx", 1, near, "split_tx", keep.reshape(shape), swap_reps(send).reshape(shape))
    else:
        (grad,) = vmem_call(back_kernel, [flat], "normed_grad", qkv_weight, first_proj)
    (normed_grad,) = vmem_call(spread_kernel, [flat], "spread", order, grad)
    spread = normed_grad.reshape(group_count, chunk, channels)
    returned = exchange(spread)

    total = rep_count * tile_count
    if halves == 2:
        parts = split("ty", 0, far, "split_ty", *travel(parts, "tx", near))
        rows = sum(part.astype(F32) for part in travel(parts, "ty", far)) / total
        (weight_grad,) = vmem_call(
            join_kernel,
            [jax.ShapeDtypeStruct((rows.shape[0], 3 * channels), F32)],
            "weight_grad",
            rows,
            swap_reps(rows),
        )
    else:
        weight_grad = lax.psum_scatter(send, ("ty", "tx"), scatter_dimension=0, tiled=True)
        weight_grad = lax.psum(weight_grad, "rep") / total

    (token_grad,) = vmem_call(
        functools.partial(unpack_kernel, split_shape),
        [jax.ShapeDtypeStruct(local, BF16)],
        "token_grad",
        returned,
        tokens,
        cotangent,
    )
    token_grad = token_grad.reshape(1, *local)
    return (token_grad, weight_grad)


def solution(mesh):
    placed = (P("rep", "ty", "tx", None), P(), P("rep", "ty", "tx", None))
    return jax.shard_map(
        shards,
        mesh=mesh,
        in_specs=placed,
        out_specs=(P("rep", "ty", "tx", None), P(("ty", "tx"), None)),
        check_vma=False,
    )
```

```python
import functools

import jax
import jax.numpy as jnp
import numpy as np
from jax import lax
from jax.experimental import pallas as pl
from jax.experimental.pallas import tpu as pltpu
from jax.sharding import PartitionSpec as P

HEAD_DIM = 32
GRID = 8
EPS = 1e-05
LANES = 128
BLOCK_HEADS = LANES // HEAD_DIM
GROUP = 8

BF16 = jnp.bfloat16
F32 = jnp.float32


def matmul(a, b, contract):
    return lax.dot_general(a, b, ((contract[:1], contract[1:]), ((), ())), preferred_element_type=F32)


def normalize(pixels):
    center = pixels - jnp.mean(pixels, axis=-1, keepdims=True)
    inv_std = lax.rsqrt(jnp.mean(center * center, axis=-1, keepdims=True) + EPS)
    return center * inv_std, inv_std


def vmem_call(kernel, outs, name, *args, scratch=(), mib=8, remote=()):
    vmem = pl.BlockSpec(memory_space=pltpu.VMEM)
    hbm = pl.BlockSpec(memory_space=pltpu.HBM)
    return pl.pallas_call(
        kernel,
        out_shape=outs,
        in_specs=[hbm if index in remote else vmem for index in range(len(args))],
        out_specs=[vmem] * len(outs),
        scratch_shapes=scratch,
        compiler_params=pltpu.CompilerParams(vmem_limit_bytes=mib * 2**20),
        name=name,
    )(*args)


def in_chunks(shape, pixels):
    channels = pixels.shape[-1]
    pixels = pixels.astype(F32).reshape(*shape, channels)
    return jnp.concatenate([pixels[index] for index in range(shape[0])], axis=1)


def pack_kernel(shape, tokens_ref, cot_ref, sent_ref, tokens_buf, cot_buf, sems):
    channels = tokens_buf.shape[2]
    copies = [
        pltpu.make_async_copy(tokens_ref, tokens_buf, sems.at[0]),
        pltpu.make_async_copy(cot_ref, cot_buf, sems.at[1]),
    ]
    for copy in copies:
        copy.start()
    copies[0].wait()
    sent_ref[:, :, :channels] = normalize(in_chunks(shape, tokens_buf[...]))[0].astype(BF16)
    copies[1].wait()
    sent_ref[:, :, channels:] = in_chunks(shape, cot_buf[...]).astype(BF16)


def unpack_kernel(shape, returned_ref, tokens_ref, cot_ref, grad_ref):
    outer, tiles, size = shape
    standard, inv_std = normalize(in_chunks(shape, tokens_ref[...]))
    normed_grad = returned_ref[...].astype(F32)
    inner = (
        normed_grad
        - jnp.mean(normed_grad, axis=-1, keepdims=True)
        - standard * jnp.mean(normed_grad * standard, axis=-1, keepdims=True)
    )
    grad = in_chunks(shape, cot_ref[...]) + inv_std * inner
    rows = grad_ref.shape[0] // outer
    for index in range(outer):
        part = grad[:, index * size : (index + 1) * size].astype(BF16)
        grad_ref[index * rows : (index + 1) * rows] = part.reshape(rows, *grad_ref.shape[1:])


def window_order(pos_ref):
    count = pos_ref.shape[1]
    rows = lax.broadcasted_iota(jnp.int32, (count, count), 0)
    return jnp.where(rows == pos_ref[...], 1.0, 0.0).astype(BF16)


def half_slices(halves, side, channels):
    width = channels // halves
    return [pl.ds(pl.multiple_of(part * channels + side * width, LANES), width) for part in range(3)]


def attend(weight_ref, columns, normed, scratch, proj_ref):
    cot_ref, query_ref, key_ref, value_ref = scratch
    count, width = cot_ref.shape
    win_tokens = GRID * GRID
    scale = HEAD_DIM**-0.5

    query_ref[...] = (matmul(normed, weight_ref[:, columns[0]], (1, 0)) * scale).astype(BF16)
    key_ref[...] = matmul(normed, weight_ref[:, columns[1]], (1, 0)).astype(BF16)
    value_ref[...] = matmul(normed, weight_ref[:, columns[2]], (1, 0)).astype(BF16)

    stack_shape = (BLOCK_HEADS * win_tokens, LANES)
    own = lax.broadcasted_iota(jnp.int32, stack_shape, 0) // win_tokens == (
        lax.broadcasted_iota(jnp.int32, stack_shape, 1) // HEAD_DIM
    )
    mask = jnp.where(own, 1.0, 0.0)
    mask_low = mask.astype(BF16)

    def stack(block):
        return jnp.concatenate([block] * BLOCK_HEADS, axis=0) * mask_low

    cells = [
        (slice(row, row + win_tokens), slice(col, col + LANES))
        for row in range(0, count, win_tokens)
        for col in range(0, width, LANES)
    ]
    for first in range(0, len(cells), GROUP):
        group = cells[first : first + GROUP]
        stacks = [(stack(query_ref[row, col]), stack(cot_ref[row, col])) for row, col in group]
        raw = []
        for (row, col), (queries, cots) in zip(group, stacks):
            scores = matmul(key_ref[row, col], queries, (1, 1))
            attn_grad = matmul(value_ref[row, col], cots, (1, 1))
            raw.append((scores, attn_grad))
        low = []
        for scores, attn_grad in raw:
            exponent = jnp.exp(scores - jnp.max(scores, axis=0, keepdims=True))
            probs = exponent * (1.0 / jnp.sum(exponent, axis=0, keepdims=True))
            score_grad = probs * (attn_grad - jnp.sum(probs * attn_grad, axis=0, keepdims=True))
            low.append((probs.astype(BF16), score_grad.astype(BF16)))
        for (row, col), (probs, score_grad), (queries, cots) in zip(group, low, stacks):
            value_grad = matmul(probs, cots, (1, 0))
            key_grad = matmul(score_grad, queries, (1, 0))
            spread = matmul(score_grad, key_ref[row, col], (0, 0)) * mask
            query_grad = spread[:win_tokens]
            for head in range(1, BLOCK_HEADS):
                query_grad += spread[head * win_tokens : (head + 1) * win_tokens]
            for part, grad in enumerate((query_grad * scale, key_grad, value_grad)):
                base = part * width + col.start
                proj_ref[row, base : base + LANES] = grad.astype(BF16)


def first_kernel(halves, pos_ref, pixels_ref, weight_ref, proj_ref, normed_ref, term_ref, cot_ref, *scratch):
    channels = normed_ref.shape[1]
    side = 1 - lax.axis_index("rep") if halves > 1 else 0
    columns = half_slices(halves, side, channels)
    onehot = window_order(pos_ref)
    normed = matmul(onehot, pixels_ref[:, :channels], (1, 0)).astype(BF16)
    normed_ref[...] = normed
    start = pl.multiple_of(columns[0].start + channels, LANES)
    cot = pixels_ref[:, pl.ds(start, columns[0].size)]
    cot_ref[...] = matmul(onehot, cot, (1, 0)).astype(BF16)
    attend(weight_ref, columns, normed, (cot_ref, *scratch), proj_ref)
    term_ref[...] = matmul(normed, proj_ref[...], (0, 0)).astype(term_ref.dtype)


def input_grad(weight_ref, columns, proj_ref):
    width = columns[0].size
    return sum(
        matmul(proj_ref[:, part * width : (part + 1) * width], weight_ref[:, column], (1, 1))
        for part, column in enumerate(columns)
    )


def second_kernel(
    pos_ref, pixels_ref, weight_ref, first_ref, normed_ref, grad_ref, term_ref, proj_ref, cot_ref, *scratch
):
    channels = normed_ref.shape[1]
    side = lax.axis_index("rep")
    columns = half_slices(2, side, channels)
    start = pl.multiple_of(columns[0].start + channels, LANES)
    cot = pixels_ref[:, pl.ds(start, columns[0].size)]
    cot_ref[...] = matmul(window_order(pos_ref), cot, (1, 0)).astype(BF16)
    normed = normed_ref[...]
    attend(weight_ref, columns, normed, (cot_ref, *scratch), proj_ref)
    grad = input_grad(weight_ref, columns, proj_ref)
    grad += input_grad(weight_ref, half_slices(2, 1 - side, channels), first_ref)
    grad_ref[...] = grad.astype(BF16)
    term_ref[...] = matmul(normed, proj_ref[...], (0, 0)).astype(BF16)


def back_kernel(weight_ref, proj_ref, grad_ref):
    grad_ref[...] = matmul(proj_ref[...], weight_ref[...], (1, 1)).astype(BF16)


def spread_kernel(pos_ref, grad_ref, out_ref):
    out_ref[...] = matmul(window_order(pos_ref), grad_ref[...], (0, 0)).astype(BF16)


def join_kernel(own_ref, other_ref, out_ref):
    width = own_ref.shape[1] // 3
    side = lax.axis_index("rep")
    for ref, half in ((own_ref, side), (other_ref, 1 - side)):
        for part in range(3):
            start = pl.multiple_of((2 * part + half) * width, LANES)
            out_ref[:, pl.ds(start, width)] = ref[:, part * width : (part + 1) * width]


def swap_reps(values):
    return lax.ppermute(values, "rep", [(0, 1), (1, 0)])


def split_kernel(axis, along, count, steps, *refs):
    me = lax.axis_index(axis)
    sources, parts = refs[:count], refs[count:]
    for step, ref in zip(steps, parts):
        index = (slice(None),) * along + (me ^ step,)
        ref[...] = sum(source[index].astype(F32) for source in sources).astype(BF16)


def split(axis, along, steps, name, *sources):
    shape = sources[0].shape
    part = jax.ShapeDtypeStruct(shape[:along] + shape[along + 1 :], BF16)
    kernel = functools.partial(split_kernel, axis, along, len(sources), steps)
    return vmem_call(kernel, [part] * len(steps), name, *sources)


def travel(parts, axis, steps):
    size = len(parts)
    return [parts[0]] + [
        lax.ppermute(part, axis, [(i, i ^ step) for i in range(size)])
        for part, step in zip(parts[1:], steps[1:])
    ]


def shards(tokens, qkv_weight, cotangent):
    rep_count = lax.axis_size("rep")
    row_tiles = lax.axis_size("ty")
    col_tiles = lax.axis_size("tx")
    tile_count = row_tiles * col_tiles
    _, tile_height, tile_width, channels = tokens.shape
    stride_rows = row_tiles * tile_height // GRID
    stride_cols = col_tiles * tile_width // GRID
    block_rows = min(tile_height, stride_rows)
    fold_rows = stride_rows // block_rows
    col_groups = tile_width // stride_cols
    outer_rows = tile_height // block_rows
    samples = rep_count if rep_count == 2 and fold_rows == 1 else 1
    group_count = tile_count * samples
    digits = {"rep": samples, "z": row_tiles // 2, "row": 2, "y": col_tiles // 2, "column": 2}
    natural = list(digits)
    turned = ["column", "y", "row", "rep", "z"] if samples == 2 else natural
    devices = np.arange(group_count).reshape(list(digits.values()))
    devices = devices.transpose([natural.index(name) for name in turned]).reshape(-1).tolist()
    groups = [[rep * tile_count + device for device in devices] for rep in range(rep_count // samples)]
    exchange = functools.partial(
        lax.all_to_all,
        axis_name=("rep", "ty", "tx"),
        split_axis=0,
        concat_axis=0,
        tiled=True,
        axis_index_groups=groups,
    )
    inner_rows = block_rows // group_count
    chunk = outer_rows * inner_rows * tile_width
    count = group_count * chunk

    dims = [(name, digits[name]) for name in turned]
    dims += [("outer", outer_rows), ("inner", inner_rows), ("group", col_groups), ("col", stride_cols)]
    names = [name for name, _ in dims]
    window = ["rep", "inner", "col"] + ["row"] * (fold_rows == 2)
    token = [name for name in names if name not in window]
    order = np.arange(count).reshape([size for _, size in dims])
    order = order.transpose([names.index(name) for name in window + token]).reshape(count)
    pos = np.zeros((1, count), np.int32)
    pos[0, order] = np.arange(count)

    local = (tile_height, tile_width, channels)
    split_shape = (outer_rows, group_count, inner_rows * tile_width)
    tokens, cotangent = tokens.reshape(local), cotangent.reshape(local)
    (sent,) = vmem_call(
        functools.partial(pack_kernel, split_shape),
        [jax.ShapeDtypeStruct((group_count, chunk, 2 * channels), BF16)],
        "pack",
        pltpu.with_memory_space_constraint(tokens, pltpu.HBM),
        pltpu.with_memory_space_constraint(cotangent, pltpu.HBM),
        scratch=[
            pltpu.VMEM(local, BF16),
            pltpu.VMEM(local, BF16),
            pltpu.SemaphoreType.DMA((2,)),
        ],
        remote=(0, 1),
    )
    pixels = exchange(sent)
    pixels = pixels.reshape(count, 2 * channels)

    halves = samples
    width = channels // halves
    order = jnp.asarray(pos)
    flat = jax.ShapeDtypeStruct((count, channels), BF16)
    proj = jax.ShapeDtypeStruct((count, 3 * width), BF16)
    term = jax.ShapeDtypeStruct((channels, 3 * width), BF16 if halves == 2 else F32)
    scratch = [pltpu.VMEM((count, width), BF16)] * 4
    first_proj, normed, send = vmem_call(
        functools.partial(first_kernel, halves),
        [proj, flat, term],
        "first_heads",
        order,
        pixels,
        qkv_weight,
        scratch=scratch,
        mib=16,
    )
    if halves == 2:
        grad, keep = vmem_call(
            second_kernel,
            [flat, term],
            "second_heads",
            order,
            pixels,
            qkv_weight,
            first_proj,
            normed,
            scratch=[pltpu.VMEM((count, 3 * width), BF16)] + scratch,
            mib=16,
        )
        near = tuple(range(col_tiles))
        far = tuple(range(row_tiles))
        shape = (row_tiles, col_tiles, channels // tile_count, 3 * width)
        parts = split("tx", 1, near, "split_tx", keep.reshape(shape), swap_reps(send).reshape(shape))
    else:
        (grad,) = vmem_call(back_kernel, [flat], "normed_grad", qkv_weight, first_proj)
    (normed_grad,) = vmem_call(spread_kernel, [flat], "spread", order, grad)
    spread = normed_grad.reshape(group_count, chunk, channels)
    returned = exchange(spread)

    total = rep_count * tile_count
    if halves == 2:
        parts = split("ty", 0, far, "split_ty", *travel(parts, "tx", near))
        rows = sum(part.astype(F32) for part in travel(parts, "ty", far)) / total
        (weight_grad,) = vmem_call(
            join_kernel,
            [jax.ShapeDtypeStruct((rows.shape[0], 3 * channels), F32)],
            "weight_grad",
            rows,
            swap_reps(rows),
        )
    else:
        weight_grad = lax.psum_scatter(send, ("ty", "tx"), scatter_dimension=0, tiled=True)
        weight_grad = lax.psum(weight_grad, "rep") / total

    (token_grad,) = vmem_call(
        functools.partial(unpack_kernel, split_shape),
        [jax.ShapeDtypeStruct(local, BF16)],
        "token_grad",
        returned,
        tokens,
        cotangent,
    )
    token_grad = token_grad.reshape(1, *local)
    return (token_grad, weight_grad)


def solution(mesh):
    placed = (P("rep", "ty", "tx", None), P(), P("rep", "ty", "tx", None))
    return jax.shard_map(
        shards,
        mesh=mesh,
        in_specs=placed,
        out_specs=(P("rep", "ty", "tx", None), P(("ty", "tx"), None)),
        check_vma=False,
    )
```

```python
import functools

import jax
import jax.numpy as jnp
import numpy as np
from jax import lax
from jax.experimental import pallas as pl
from jax.experimental.pallas import tpu as pltpu
from jax.sharding import PartitionSpec as P

HEAD_DIM = 32
GRID = 8
EPS = 1e-05
LANES = 128
BLOCK_HEADS = LANES // HEAD_DIM
GROUP = 8

BF16 = jnp.bfloat16
F32 = jnp.float32


def matmul(a, b, contract):
    return lax.dot_general(a, b, ((contract[:1], contract[1:]), ((), ())), preferred_element_type=F32)


def normalize(pixels):
    center = pixels - jnp.mean(pixels, axis=-1, keepdims=True)
    inv_std = lax.rsqrt(jnp.mean(center * center, axis=-1, keepdims=True) + EPS)
    return center * inv_std, inv_std


def vmem_call(kernel, outs, name, *args, scratch=(), mib=8, remote=()):
    vmem = pl.BlockSpec(memory_space=pltpu.VMEM)
    hbm = pl.BlockSpec(memory_space=pltpu.HBM)
    return pl.pallas_call(
        kernel,
        out_shape=outs,
        in_specs=[hbm if index in remote else vmem for index in range(len(args))],
        out_specs=[vmem] * len(outs),
        scratch_shapes=scratch,
        compiler_params=pltpu.CompilerParams(vmem_limit_bytes=mib * 2**20),
        name=name,
    )(*args)


def in_chunks(shape, pixels):
    channels = pixels.shape[-1]
    pixels = pixels.astype(F32).reshape(*shape, channels)
    return jnp.concatenate([pixels[index] for index in range(shape[0])], axis=1)


def pack_kernel(shape, tokens_ref, cot_ref, sent_ref, tokens_buf, cot_buf, sems):
    channels = tokens_buf.shape[2]
    copies = [
        pltpu.make_async_copy(tokens_ref, tokens_buf, sems.at[0]),
        pltpu.make_async_copy(cot_ref, cot_buf, sems.at[1]),
    ]
    for copy in copies:
        copy.start()
    copies[0].wait()
    sent_ref[:, :, :channels] = normalize(in_chunks(shape, tokens_buf[...]))[0].astype(BF16)
    copies[1].wait()
    cot = cot_buf[...].reshape(*shape, channels)
    sent_ref[:, :, channels:] = jnp.concatenate([cot[index] for index in range(shape[0])], axis=1)


def unpack_kernel(shape, returned_ref, tokens_ref, cot_ref, grad_ref):
    outer, tiles, size = shape
    standard, inv_std = normalize(in_chunks(shape, tokens_ref[...]))
    normed_grad = returned_ref[...].astype(F32)
    inner = (
        normed_grad
        - jnp.mean(normed_grad, axis=-1, keepdims=True)
        - standard * jnp.mean(normed_grad * standard, axis=-1, keepdims=True)
    )
    grad = in_chunks(shape, cot_ref[...]) + inv_std * inner
    rows = grad_ref.shape[0] // outer
    for index in range(outer):
        part = grad[:, index * size : (index + 1) * size].astype(BF16)
        grad_ref[index * rows : (index + 1) * rows] = part.reshape(rows, *grad_ref.shape[1:])


def window_order(pos_ref):
    count = pos_ref.shape[1]
    rows = lax.broadcasted_iota(jnp.int32, (count, count), 0)
    return jnp.where(rows == pos_ref[...], 1.0, 0.0).astype(BF16)


def half_slices(halves, side, channels):
    width = channels // halves
    return [pl.ds(pl.multiple_of(part * channels + side * width, LANES), width) for part in range(3)]


def attend(weight_ref, columns, normed, scratch, proj_ref):
    cot_ref, query_ref, key_ref, value_ref = scratch
    count, width = cot_ref.shape
    win_tokens = GRID * GRID
    scale = HEAD_DIM**-0.5

    query_ref[...] = (matmul(normed, weight_ref[:, columns[0]], (1, 0)) * scale).astype(BF16)
    key_ref[...] = matmul(normed, weight_ref[:, columns[1]], (1, 0)).astype(BF16)
    value_ref[...] = matmul(normed, weight_ref[:, columns[2]], (1, 0)).astype(BF16)

    stack_shape = (BLOCK_HEADS * win_tokens, LANES)
    own = lax.broadcasted_iota(jnp.int32, stack_shape, 0) // win_tokens == (
        lax.broadcasted_iota(jnp.int32, stack_shape, 1) // HEAD_DIM
    )
    mask = jnp.where(own, 1.0, 0.0)
    mask_low = mask.astype(BF16)

    def stack(block):
        return jnp.concatenate([block] * BLOCK_HEADS, axis=0) * mask_low

    cells = [
        (slice(row, row + win_tokens), slice(col, col + LANES))
        for row in range(0, count, win_tokens)
        for col in range(0, width, LANES)
    ]
    for first in range(0, len(cells), GROUP):
        group = cells[first : first + GROUP]
        stacks = [(stack(query_ref[row, col]), stack(cot_ref[row, col])) for row, col in group]
        raw = []
        for (row, col), (queries, cots) in zip(group, stacks):
            scores = matmul(key_ref[row, col], queries, (1, 1))
            attn_grad = matmul(value_ref[row, col], cots, (1, 1))
            raw.append((scores, attn_grad))
        low = []
        for scores, attn_grad in raw:
            exponent = jnp.exp(scores - jnp.max(scores, axis=0, keepdims=True))
            probs = exponent * (1.0 / jnp.sum(exponent, axis=0, keepdims=True))
            score_grad = probs * (attn_grad - jnp.sum(probs * attn_grad, axis=0, keepdims=True))
            low.append((probs.astype(BF16), score_grad.astype(BF16)))
        for (row, col), (probs, score_grad), (queries, cots) in zip(group, low, stacks):
            value_grad = matmul(probs, cots, (1, 0))
            key_grad = matmul(score_grad, queries, (1, 0))
            spread = matmul(score_grad, key_ref[row, col], (0, 0)) * mask
            query_grad = spread[:win_tokens]
            for head in range(1, BLOCK_HEADS):
                query_grad += spread[head * win_tokens : (head + 1) * win_tokens]
            for part, grad in enumerate((query_grad * scale, key_grad, value_grad)):
                base = part * width + col.start
                proj_ref[row, base : base + LANES] = grad.astype(BF16)


def first_kernel(halves, pos_ref, pixels_ref, weight_ref, proj_ref, normed_ref, term_ref, cot_ref, *scratch):
    channels = normed_ref.shape[1]
    side = 1 - lax.axis_index("rep") if halves > 1 else 0
    columns = half_slices(halves, side, channels)
    onehot = window_order(pos_ref)
    normed = matmul(onehot, pixels_ref[:, :channels], (1, 0)).astype(BF16)
    normed_ref[...] = normed
    start = pl.multiple_of(columns[0].start + channels, LANES)
    cot = pixels_ref[:, pl.ds(start, columns[0].size)]
    cot_ref[...] = matmul(onehot, cot, (1, 0)).astype(BF16)
    attend(weight_ref, columns, normed, (cot_ref, *scratch), proj_ref)
    term_ref[...] = matmul(normed, proj_ref[...], (0, 0)).astype(term_ref.dtype)


def input_grad(weight_ref, columns, proj_ref):
    width = columns[0].size
    return sum(
        matmul(proj_ref[:, part * width : (part + 1) * width], weight_ref[:, column], (1, 1))
        for part, column in enumerate(columns)
    )


def second_kernel(
    pos_ref, pixels_ref, weight_ref, first_ref, normed_ref, grad_ref, term_ref, proj_ref, cot_ref, *scratch
):
    channels = normed_ref.shape[1]
    side = lax.axis_index("rep")
    columns = half_slices(2, side, channels)
    start = pl.multiple_of(columns[0].start + channels, LANES)
    cot = pixels_ref[:, pl.ds(start, columns[0].size)]
    cot_ref[...] = matmul(window_order(pos_ref), cot, (1, 0)).astype(BF16)
    normed = normed_ref[...]
    attend(weight_ref, columns, normed, (cot_ref, *scratch), proj_ref)
    grad = input_grad(weight_ref, columns, proj_ref)
    grad += input_grad(weight_ref, half_slices(2, 1 - side, channels), first_ref)
    grad_ref[...] = grad.astype(BF16)
    term_ref[...] = matmul(normed, proj_ref[...], (0, 0)).astype(BF16)


def back_kernel(weight_ref, proj_ref, grad_ref):
    grad_ref[...] = matmul(proj_ref[...], weight_ref[...], (1, 1)).astype(BF16)


def spread_kernel(pos_ref, grad_ref, out_ref):
    out_ref[...] = matmul(window_order(pos_ref), grad_ref[...], (0, 0)).astype(BF16)


def join_kernel(own_ref, other_ref, out_ref):
    width = own_ref.shape[1] // 3
    side = lax.axis_index("rep")
    for ref, half in ((own_ref, side), (other_ref, 1 - side)):
        for part in range(3):
            start = pl.multiple_of((2 * part + half) * width, LANES)
            out_ref[:, pl.ds(start, width)] = ref[:, part * width : (part + 1) * width]


def swap_reps(values):
    return lax.ppermute(values, "rep", [(0, 1), (1, 0)])


def split_kernel(axis, along, count, steps, *refs):
    me = lax.axis_index(axis)
    sources, parts = refs[:count], refs[count:]
    for step, ref in zip(steps, parts):
        index = (slice(None),) * along + (me ^ step,)
        ref[...] = sum(source[index].astype(F32) for source in sources).astype(BF16)


def split(axis, along, steps, name, *sources):
    shape = sources[0].shape
    part = jax.ShapeDtypeStruct(shape[:along] + shape[along + 1 :], BF16)
    kernel = functools.partial(split_kernel, axis, along, len(sources), steps)
    return vmem_call(kernel, [part] * len(steps), name, *sources)


def travel(parts, axis, steps):
    size = len(parts)
    return [parts[0]] + [
        lax.ppermute(part, axis, [(i, i ^ step) for i in range(size)])
        for part, step in zip(parts[1:], steps[1:])
    ]


def shards(tokens, qkv_weight, cotangent):
    rep_count = lax.axis_size("rep")
    row_tiles = lax.axis_size("ty")
    col_tiles = lax.axis_size("tx")
    tile_count = row_tiles * col_tiles
    _, tile_height, tile_width, channels = tokens.shape
    stride_rows = row_tiles * tile_height // GRID
    stride_cols = col_tiles * tile_width // GRID
    block_rows = min(tile_height, stride_rows)
    fold_rows = stride_rows // block_rows
    col_groups = tile_width // stride_cols
    outer_rows = tile_height // block_rows
    samples = rep_count if rep_count == 2 and fold_rows == 1 else 1
    group_count = tile_count * samples
    digits = {"rep": samples, "z": row_tiles // 2, "row": 2, "y": col_tiles // 2, "column": 2}
    natural = list(digits)
    turned = ["column", "y", "row", "rep", "z"] if samples == 2 else natural
    devices = np.arange(group_count).reshape(list(digits.values()))
    devices = devices.transpose([natural.index(name) for name in turned]).reshape(-1).tolist()
    groups = [[rep * tile_count + device for device in devices] for rep in range(rep_count // samples)]
    exchange = functools.partial(
        lax.all_to_all,
        axis_name=("rep", "ty", "tx"),
        split_axis=0,
        concat_axis=0,
        tiled=True,
        axis_index_groups=groups,
    )
    inner_rows = block_rows // group_count
    chunk = outer_rows * inner_rows * tile_width
    count = group_count * chunk

    dims = [(name, digits[name]) for name in turned]
    dims += [("outer", outer_rows), ("inner", inner_rows), ("group", col_groups), ("col", stride_cols)]
    names = [name for name, _ in dims]
    window = ["rep", "inner", "col"] + ["row"] * (fold_rows == 2)
    token = [name for name in names if name not in window]
    order = np.arange(count).reshape([size for _, size in dims])
    order = order.transpose([names.index(name) for name in window + token]).reshape(count)
    pos = np.zeros((1, count), np.int32)
    pos[0, order] = np.arange(count)

    local = (tile_height, tile_width, channels)
    split_shape = (outer_rows, group_count, inner_rows * tile_width)
    tokens, cotangent = tokens.reshape(local), cotangent.reshape(local)
    (sent,) = vmem_call(
        functools.partial(pack_kernel, split_shape),
        [jax.ShapeDtypeStruct((group_count, chunk, 2 * channels), BF16)],
        "pack",
        pltpu.with_memory_space_constraint(tokens, pltpu.HBM),
        pltpu.with_memory_space_constraint(cotangent, pltpu.HBM),
        scratch=[
            pltpu.VMEM(local, BF16),
            pltpu.VMEM(local, BF16),
            pltpu.SemaphoreType.DMA((2,)),
        ],
        remote=(0, 1),
    )
    pixels = exchange(sent)
    pixels = pixels.reshape(count, 2 * channels)

    halves = samples
    width = channels // halves
    order = jnp.asarray(pos)
    flat = jax.ShapeDtypeStruct((count, channels), BF16)
    proj = jax.ShapeDtypeStruct((count, 3 * width), BF16)
    term = jax.ShapeDtypeStruct((channels, 3 * width), BF16 if halves == 2 else F32)
    scratch = [pltpu.VMEM((count, width), BF16)] * 4
    first_proj, normed, send = vmem_call(
        functools.partial(first_kernel, halves),
        [proj, flat, term],
        "first_heads",
        order,
        pixels,
        qkv_weight,
        scratch=scratch,
        mib=16,
    )
    if halves == 2:
        grad, keep = vmem_call(
            second_kernel,
            [flat, term],
            "second_heads",
            order,
            pixels,
            qkv_weight,
            first_proj,
            normed,
            scratch=[pltpu.VMEM((count, 3 * width), BF16)] + scratch,
            mib=16,
        )
        near = tuple(range(col_tiles))
        far = tuple(range(row_tiles))
        shape = (row_tiles, col_tiles, channels // tile_count, 3 * width)
        parts = split("tx", 1, near, "split_tx", keep.reshape(shape), swap_reps(send).reshape(shape))
    else:
        (grad,) = vmem_call(back_kernel, [flat], "normed_grad", qkv_weight, first_proj)
    (normed_grad,) = vmem_call(spread_kernel, [flat], "spread", order, grad)
    spread = normed_grad.reshape(group_count, chunk, channels)
    returned = exchange(spread)

    total = rep_count * tile_count
    if halves == 2:
        parts = split("ty", 0, far, "split_ty", *travel(parts, "tx", near))
        rows = sum(part.astype(F32) for part in travel(parts, "ty", far)) / total
        (weight_grad,) = vmem_call(
            join_kernel,
            [jax.ShapeDtypeStruct((rows.shape[0], 3 * channels), F32)],
            "weight_grad",
            rows,
            swap_reps(rows),
        )
    else:
        weight_grad = lax.psum_scatter(send, ("ty", "tx"), scatter_dimension=0, tiled=True)
        weight_grad = lax.psum(weight_grad, "rep") / total

    (token_grad,) = vmem_call(
        functools.partial(unpack_kernel, split_shape),
        [jax.ShapeDtypeStruct(local, BF16)],
        "token_grad",
        returned,
        tokens,
        cotangent,
    )
    token_grad = token_grad.reshape(1, *local)
    return (token_grad, weight_grad)


def solution(mesh):
    placed = (P("rep", "ty", "tx", None), P(), P("rep", "ty", "tx", None))
    return jax.shard_map(
        shards,
        mesh=mesh,
        in_specs=placed,
        out_specs=(P("rep", "ty", "tx", None), P(("ty", "tx"), None)),
        check_vma=False,
    )
```
